256 devices in a mesh: view: 8 (over z_hi, core), gz: 32 (over z_lo, y, x).
Axes of the slice: x: 4, y: 4, z: 8 (z_hi: 4, z_lo: 2; z = z_hi * 2 + z_lo), core: 2. Of those that a mesh axis runs over, the one named last changes fastest.
Arguments:
- estimate: float32 [1536, 128, 128], P('gz'), may hold values from 0.5 to 2
- measured: float32 [8, 1536, 128, 128], P('view', 'gz'), may hold values from 0.3 to 3
- lateral_x: float32 [8, 128, 128], P('view'), may hold values from 0 to 0.5, as said below
- lateral_y: float32 [8, 128, 128], P('view'), may hold values from 0 to 0.5, as said below
- depth_taps: float32 [8, 33], P('view'), may hold values from 0.01 to 0.06
Outputs:
- updated: float32 [1536, 128, 128], P('gz')
The draws below stay inside these ranges and needn't reach their ends.
Inputs may be any that keep to these rules, and one draw needn't show every extreme that they name: `lateral_x`: nonnegative entries. `lateral_y`: nonnegative entries.
All inputs are finite; a program needn't handle non-finite values.
Results may differ from the reference program's by a relative error of at most 0.0001.
Values sent between devices are 32-bit elements; how exact they have to be, the bound alone decides.
No kernel may reach another device: no remote copies, remote signals or barrier semaphores. Data moves between devices by JAX's collectives and lax.ppermute only.
A program may use at most 64 MiB of HBM per device.

```python
import math
import jax
import jax.numpy as jnp
from jax import lax

NX = 128
NY = 128
DEPTH = 33
HALF = 16
ITERS = 2
VIEWS = 8
NZ = 1536


def banded_blur(key, count, width):
    first, second = jax.random.split(key)
    spread = jnp.exp(jax.random.uniform(first, (count, 1, 1), jnp.float32, jnp.log(1.2), jnp.log(3.0)))
    rows = jnp.arange(width)[:, None]
    cols = jnp.arange(width)[None, :]
    offset = (rows - cols).astype(jnp.float32)
    rough = jax.random.uniform(second, (count, width, width), jnp.float32, 0.5, 1.5)
    shape_value = jnp.exp(-offset * offset / (2.0 * spread * spread)) * rough / (2.5 * spread)
    return jnp.where(jnp.abs(offset) <= 6.0, shape_value, 0.0).astype(jnp.float32)


def draw_lateral_x(key, part):
    key = jax.random.fold_in(key, 11)
    return banded_blur(key, VIEWS, NX)


def draw_lateral_y(key, part):
    key = jax.random.fold_in(key, 23)
    return banded_blur(key, VIEWS, NY)


def level_of(key, dims, shards, least, top_value):
    level = 1.0
    for position, parts in shards:
        heights = jax.random.uniform(jax.random.fold_in(jax.random.fold_in(key, 6), position), (parts,), jnp.float32, least / len(shards), top_value / len(shards))
        level = level * jnp.repeat(jnp.exp(heights), dims[position] // parts).reshape((-1,) + (1,) * (len(dims) - 1 - position))
    return level


def setup_inputs(seed: int = 0) -> dict:
    key_list = jax.random.split(jax.random.key(seed), 6)
    estimate = jnp.clip(jnp.exp(math.log(2.0) - 1.3862944 * jax.random.uniform(key_list[0], (NZ, NX, NY), jnp.float32) ** level_of(key_list[0], (NZ, NX, NY), ((0, 32),), -0.2, 0.2)), 0.5, 2.0)
    measured = jnp.clip(jnp.exp(math.log(3.0) - 2.3025851 * jax.random.uniform(key_list[1], (VIEWS, NZ, NX, NY), jnp.float32) ** level_of(key_list[1], (VIEWS, NZ, NX, NY), ((0, 8), (1, 32)), -0.2, 0.2)), 0.3, 3.0)
    lateral_x = draw_lateral_x(jax.random.fold_in(key_list[5], 71), 0)
    lateral_y = draw_lateral_y(jax.random.fold_in(key_list[5], 71), 0)
    depth_taps = jnp.clip(jnp.exp(math.log(0.06) - 1.7917595 * jax.random.uniform(key_list[4], (VIEWS, DEPTH), jnp.float32) ** level_of(key_list[4], (VIEWS, DEPTH), ((0, 8),), -0.2, 0.2)), 0.01, 0.06)
    return dict(estimate=estimate, measured=measured, lateral_x=lateral_x, lateral_y=lateral_y, depth_taps=depth_taps)


def lateral_forward(field, across, along):
    step = jnp.einsum("zxy,ax->zay", field, across, precision=lax.Precision.HIGHEST)
    return jnp.einsum("zay,by->zab", step, along, precision=lax.Precision.HIGHEST)


def lateral_adjoint(field, across, along):
    step = jnp.einsum("zab,ax->zxb", field, across, precision=lax.Precision.HIGHEST)
    return jnp.einsum("zxb,by->zxy", step, along, precision=lax.Precision.HIGHEST)


def depth_blur(padded, taps, count):
    total = jnp.zeros((count,) + padded.shape[1:], jnp.float32)
    for shift in range(DEPTH):
        total = total + taps[shift] * padded[shift:shift + count]
    return total


def depth_adjoint(padded, taps, count):
    total = jnp.zeros((count,) + padded.shape[1:], jnp.float32)
    for shift in range(DEPTH):
        begin = 2 * HALF - shift
        total = total + taps[shift] * padded[begin:begin + count]
    return total


def reference(estimate, measured, lateral_x, lateral_y, depth_taps):
    updated = estimate
    rim = ((HALF, HALF), (0, 0), (0, 0))
    for update in range(ITERS):
        log_sum = jnp.zeros_like(updated)
        for view in range(VIEWS):
            smooth = lateral_forward(updated, lateral_x[view], lateral_y[view])
            blurred = depth_blur(jnp.pad(smooth, rim), depth_taps[view], NZ)
            ratio = measured[view] / blurred
            back = depth_adjoint(jnp.pad(ratio, rim), depth_taps[view], NZ)
            factor = lateral_adjoint(back, lateral_x[view], lateral_y[view])
            log_sum = log_sum + jnp.log(factor)
        updated = updated * jnp.exp(log_sum / VIEWS)
    return updated
```

```python
import jax
import jax.numpy as jnp
from jax import lax
from jax.experimental import pallas as pl
from jax.experimental.pallas import tpu as pltpu
from jax.sharding import PartitionSpec as P

DEPTH = 33
HALF = 16
N = 128
SLAB = 48
FAR = 2 * HALF
F32 = jnp.float32
BF16 = jnp.bfloat16
MIB = 1024 * 1024


def split(x):
    hi = x.astype(BF16)
    return hi, (x - hi.astype(F32)).astype(BF16)


def split_matrix(m):
    hi = lax.reduce_precision(m, 8, 7)
    return hi.astype(BF16), lax.reduce_precision(m - hi, 8, 7).astype(BF16)


def left_operand(m):
    hi, lo = split_matrix(m)
    return jnp.concatenate([jnp.concatenate([hi, hi], 1), jnp.concatenate([lo, lo], 1)], 0)


def right_operand(m):
    hi, lo = split_matrix(m)
    return jnp.concatenate([jnp.concatenate([hi, lo], 1), jnp.concatenate([hi, lo], 1)], 0)


def left_product(operand, x):
    hi, lo = split(x)
    out = jnp.dot(operand, jnp.concatenate([hi, lo], 0), preferred_element_type=F32)
    rows = operand.shape[0] // 2
    return out[:rows] + out[rows:]


def right_product(x, operand):
    hi, lo = split(x)
    out = jnp.dot(jnp.concatenate([hi, lo], 1), operand, preferred_element_type=F32)
    cols = operand.shape[1] // 2
    return out[:, :cols] + out[:, cols:]


def two_sided(planes, left, right):
    both = left_product(left, jnp.concatenate(planes, 1))
    rows = jnp.concatenate([both[:, :N], both[:, N:]], 0)
    return right_product(rows, right)


def region_plane(refs, z):
    blocks = []
    for ref in refs:
        if len(ref.shape) == 3:
            blocks.append(ref[z])
        else:
            blocks.extend(ref[p, z] for p in range(ref.shape[0]))
    return jnp.concatenate(blocks, 0) if len(blocks) > 1 else blocks[0]


def lateral_kernel(counts, *refs):
    total = sum(c for c, _ in counts)
    ins, (left_ref, right_ref), outs = refs[:total], refs[total : total + 2], refs[total + 2 :]
    left = left_ref[...]
    right = right_ref[...]
    at = 0
    for (count, planes), out in zip(counts, outs):
        region = ins[at : at + count]
        at += count

        @pl.loop(0, planes // 4)
        def _(i, region=region, out=out):
            for j in range(2):
                z = 4 * i + 2 * j
                res = two_sided([region_plane(region, z), region_plane(region, z + 1)], left, right)
                out[pl.ds(pl.multiple_of(z * N, 2 * N), 2 * N), :] = res


def lateral(regions, left, right):
    counts = []
    ins = []
    for region in regions:
        ref = region[0]
        counts.append((len(region), ref.shape[0] if ref.ndim == 3 else ref.shape[1]))
        ins.extend(region)
    planes = sum(p for _, p in counts)
    return pl.pallas_call(
        lambda *refs: lateral_kernel(counts, *refs),
        out_shape=[jax.ShapeDtypeStruct((p * N, N), F32) for _, p in counts],
        in_specs=[pl.BlockSpec(memory_space=pltpu.VMEM)] * (len(ins) + 2),
        out_specs=[pl.BlockSpec(memory_space=pltpu.VMEM)] * len(counts),
        compiler_params=pltpu.CompilerParams(vmem_limit_bytes=20 * MIB),
        cost_estimate=pl.CostEstimate(flops=planes * 16 * N**3, bytes_accessed=planes * 8 * N * N, transcendentals=0),
        name="lateral",
    )(*ins, left, right)


def middle_kernel(sb, so, sa, mb, mo, ma, tf_ref, ta_ref, left_ref, right_ref, own, other, back):
    tf = tf_ref[...]
    ta = ta_ref[...]

    def rows(refs, a):
        return jnp.concatenate([r[pl.ds(a, r.shape[0] // N, stride=N), :] for r in refs], 0)

    def pair(refs, a):
        return jnp.concatenate([rows(refs, a), rows(refs, a + 1)], 1)

    @pl.loop(0, N // 4)
    def _(i):
        for j in range(2):
            a = 4 * i + 2 * j
            blurred = left_product(tf, pair((sb, so, sa), a))
            recorded = pair((mb, mo, ma), a)
            ratio = jnp.where(recorded > 0, recorded / blurred, 0.0)
            res = left_product(ta, ratio)
            back[pl.ds(a, SLAB, stride=N), :] = res[:, :N]
            back[pl.ds(a + 1, SLAB, stride=N), :] = res[:, N:]

    left = left_ref[...]
    right = right_ref[...]

    @pl.loop(0, SLAB // 4)
    def _(i):
        for j in range(2):
            z = 4 * i + 2 * j
            at = pl.multiple_of(z * N, 2 * N)
            logs = jnp.log(two_sided([back[pl.ds(at, N), :], back[pl.ds(at + N, N), :]], left, right))
            for k in range(2):
                for p in range(8):
                    own[p, z + k] = logs[k * N + 8 * p : k * N + 8 * p + 8]
                    other[p, z + k] = logs[k * N + 64 + 8 * p : k * N + 64 + 8 * p + 8]


def middle(smooth, recorded, tf, ta, left, right):
    ins = [*smooth, *[r.reshape(-1, N) for r in recorded], tf, ta, left, right]
    half = jax.ShapeDtypeStruct((8, SLAB, 8, N), F32)
    return pl.pallas_call(
        middle_kernel,
        out_shape=[half, half],
        in_specs=[pl.BlockSpec(memory_space=pltpu.VMEM)] * len(ins),
        out_specs=[pl.BlockSpec(memory_space=pltpu.VMEM)] * 2,
        scratch_shapes=[pltpu.VMEM((SLAB * N, N), F32)],
        compiler_params=pltpu.CompilerParams(vmem_limit_bytes=28 * MIB),
        cost_estimate=pl.CostEstimate(flops=8 * 10**9, bytes_accessed=15 * MIB, transcendentals=SLAB * N * N),
        name="middle",
    )(*ins)


def place_kernel(starts, *refs):
    out = refs[-1]
    at = 0
    for ref in refs[:-1]:
        for p in range(ref.shape[0]):
            begin = pl.multiple_of(starts[at], 8)
            out[:, pl.ds(begin, 8), :] = ref[p]
            at += 1


def place(starts, pieces):
    return pl.pallas_call(
        place_kernel,
        out_shape=jax.ShapeDtypeStruct((SLAB, N, N), F32),
        in_specs=[pl.BlockSpec(memory_space=pltpu.SMEM)] + [pl.BlockSpec(memory_space=pltpu.VMEM)] * len(pieces),
        out_specs=pl.BlockSpec(memory_space=pltpu.VMEM),
        compiler_params=pltpu.CompilerParams(vmem_limit_bytes=16 * MIB),
        name="place",
    )(starts, *pieces)


def to_core(x):
    return lax.ppermute(x, "view", [(i, i ^ 1) for i in range(8)])


def to_next(x):
    return lax.ppermute(x, "view", [(i, (i + 2) % 8) for i in range(8)])


def to_prev(x):
    return lax.ppermute(x, "view", [(i, (i - 2) % 8) for i in range(8)])


def up(x):
    n = lax.axis_size("gz")
    return lax.ppermute(x, "gz", [(i, i + 1) for i in range(n - 1)])


def down(x):
    n = lax.axis_size("gz")
    return lax.ppermute(x, "gz", [(i + 1, i) for i in range(n - 1)])


def reduce_chunk(other, own):
    total = own + to_core(other)
    from_prev = to_next(total[0:2])
    from_next = to_prev(total[2:4])
    fwd_next = total[4:5] + from_prev[0:1]
    fwd_prev = total[5:6] + from_next[0:1]
    last_a = to_next(fwd_next)
    last_b = to_prev(fwd_prev)
    a = total[6:7] + from_next[1:2] + last_a
    b = total[7:8] + from_prev[1:2] + last_b
    return jnp.concatenate([a, b], 0)


def on_device(estimate, measured, lateral_x, lateral_y, depth_taps):
    view = lax.axis_index("view")
    core = lax.rem(view, 2)
    chip = lax.div(view, 2)
    recorded = measured[0]
    mx = lateral_x[0]
    my = lateral_y[0]
    taps = depth_taps[0]

    half = lax.dynamic_slice_in_dim(estimate, core * 64, 64, axis=1)
    before = up(half[SLAB - FAR :])
    after = down(half[:FAR])
    before, after, recorded = lax.optimization_barrier((before, after, recorded))
    rec_before = up(recorded[SLAB - HALF :])
    rec_after = down(recorded[:HALF])
    before2, after2 = to_core(before), to_core(after)

    nxt, prv, opp = (chip + 1) % 4, (chip + 3) % 4, (chip + 2) % 4
    order = jnp.stack([2 * opp, 2 * nxt + 1, 2 * opp + 1, 2 * prv, 2 * nxt, 2 * prv + 1, 2 * chip, 2 * chip + 1])
    starts = jnp.concatenate([core * 64 + 8 * order, (1 - core) * 64 + 8 * order]).astype(jnp.int32)
    xt = mx.T
    xt_pieces = jnp.concatenate([lax.dynamic_slice_in_dim(xt, starts[p], 8, axis=0) for p in range(16)], 0)
    x_pieces = xt_pieces.T
    x_halves = jnp.roll(mx, core * 64, axis=1)

    diag = jnp.arange(112)[None, :] - jnp.arange(80)[:, None]
    shift = jnp.arange(DEPTH)[:, None, None]
    toeplitz = jnp.sum(jnp.where(diag[None] == shift, taps[:, None, None], 0.0), 0)
    adjoint = jnp.sum(jnp.where(diag[None, :SLAB, :80] == shift, taps[::-1][:, None, None], 0.0), 0)
    tf = left_operand(toeplitz)
    ta = left_operand(adjoint)
    fwd_y = right_operand(my.T)
    adj_y = right_operand(my)
    adj_x = left_operand(xt_pieces)

    def middle_of(smooth):
        return middle(smooth, (rec_before, recorded, rec_after), tf, ta, adj_x, adj_y)

    mine = jnp.stack(
        [lax.dynamic_slice_in_dim(estimate, starts[6 + k], 8, axis=1) for k in range(2)], 0
    )

    (smooth_own,) = lateral([[estimate]], left_operand(mx), fwd_y)
    smooth_b, smooth_a = lateral([[before, before2], [after, after2]], left_operand(x_halves), fwd_y)
    own, other = middle_of((smooth_b, smooth_own, smooth_a))
    mine = mine * jnp.exp(reduce_chunk(other, own) / 8.0)

    prev_c, next_c = to_next(mine), to_prev(mine)
    b0, a0 = up(mine[:, SLAB - FAR :]), down(mine[:, :FAR])
    opp_a, opp_b = to_next(prev_c[0:1]), to_prev(next_c[1:2])
    sides = jnp.concatenate([prev_c, next_c], 0)
    b1, a1 = up(sides[:, SLAB - FAR :]), down(sides[:, :FAR])
    near = jnp.concatenate([mine, sides], 0)
    near2 = to_core(near)
    opp_c = jnp.concatenate([opp_a, opp_b], 0)
    b2, a2 = up(opp_c[:, SLAB - FAR :]), down(opp_c[:, :FAR])
    opp2 = to_core(opp_c)
    ends = jnp.concatenate([b0, b1, a0, a1], 0)
    ends2 = to_core(ends)
    tail = jnp.concatenate([b2, a2], 0)
    tail2 = to_core(tail)

    x_fwd = left_operand(x_pieces)

    def in_order(near, opp_c):
        mine, prv, nxt = near[0:2], near[2:4], near[4:6]
        return [opp_c[0:1], nxt[1:2], opp_c[1:2], prv[0:1], nxt[0:1], prv[1:2], mine]

    (smooth_own,) = lateral([in_order(near, opp_c) + in_order(near2, opp2)], x_fwd, fwd_y)
    smooth_b, smooth_a = lateral(
        [
            in_order(ends[0:6], tail[0:2]) + in_order(ends2[0:6], tail2[0:2]),
            in_order(ends[6:12], tail[2:4]) + in_order(ends2[6:12], tail2[2:4]),
        ],
        x_fwd,
        fwd_y,
    )
    own, other = middle_of((smooth_b, smooth_own, smooth_a))
    mine = mine * jnp.exp(reduce_chunk(other, own) / 8.0)
    prev_c, next_c = to_next(mine), to_prev(mine)
    near = jnp.concatenate([mine, prev_c, next_c], 0)
    near2 = to_core(near)
    opp_c = jnp.concatenate([to_next(prev_c[0:1]), to_prev(next_c[1:2])], 0)
    opp2 = to_core(opp_c)
    return place(starts, in_order(near, opp_c) + in_order(near2, opp2))


def solution(mesh):
    return jax.shard_map(
        on_device,
        mesh=mesh,
        in_specs=(
            P("gz", None, None),
            P("view", "gz", None, None),
            P("view", None, None),
            P("view", None, None),
            P("view", None),
        ),
        out_specs=P("gz", None, None),
        check_vma=False,
    )
```

```python
import jax
import jax.numpy as jnp
from jax import lax
from jax.experimental import pallas as pl
from jax.experimental.pallas import tpu as pltpu
from jax.sharding import PartitionSpec as P

DEPTH = 33
HALF = 16
N = 128
SLAB = 48
FAR = 2 * HALF
F32 = jnp.float32
BF16 = jnp.bfloat16
MIB = 1024 * 1024
PITCH = 132
STEP = 16


def split(x):
    hi = x.astype(BF16)
    return hi, (x - hi.astype(F32)).astype(BF16)


def left_product(operand, x):
    hi, lo = split(x)
    out = jnp.dot(operand, jnp.concatenate([hi, lo], 0), preferred_element_type=F32)
    rows = operand.shape[0] // 2
    return out[:rows] + out[rows:]


def right_product(x, operand):
    hi, lo = split(x)
    out = jnp.dot(jnp.concatenate([hi, lo], 1), operand, preferred_element_type=F32)
    cols = operand.shape[1] // 2
    return out[:, :cols] + out[:, cols:]


def two_sided(planes, left, right):
    sides = [
        left_product(left, jnp.concatenate(planes[i : i + 2], 1)) for i in range(0, len(planes), 2)
    ]
    rows = jnp.concatenate([part for s in sides for part in (s[:, :N], s[:, N:])], 0)
    return right_product(rows, right)


def region_plane(refs, z):
    blocks = []
    for ref in refs:
        if len(ref.shape) == 3:
            blocks.append(ref[z])
        else:
            blocks.extend(ref[p, z] for p in range(ref.shape[0]))
    return jnp.concatenate(blocks, 0) if len(blocks) > 1 else blocks[0]


def lateral_kernel(counts, *refs):
    total = sum(c for c, _ in counts)
    ins, (left_ref, right_ref), outs = refs[:total], refs[total : total + 2], refs[total + 2 :]
    left = left_ref[...]
    right = right_ref[...]
    at = 0
    for (count, planes), out in zip(counts, outs):
        region = ins[at : at + count]
        at += count

        @pl.loop(0, planes // STEP)
        def _(i, region=region, out=out):
            zs = [STEP * i + j for j in range(STEP)]
            res = two_sided([region_plane(region, z) for z in zs], left, right)
            for j, z in enumerate(zs):
                out[pl.ds(z * PITCH, N), :] = res[j * N : j * N + N]


def lateral(regions, left, right):
    counts = []
    ins = []
    for region in regions:
        ref = region[0]
        counts.append((len(region), ref.shape[0] if ref.ndim == 3 else ref.shape[1]))
        ins.extend(region)
    planes = sum(p for _, p in counts)
    return pl.pallas_call(
        lambda *refs: lateral_kernel(counts, *refs),
        out_shape=[jax.ShapeDtypeStruct((p * PITCH, N), F32) for _, p in counts],
        in_specs=[pl.BlockSpec(memory_space=pltpu.VMEM)] * (len(ins) + 2),
        out_specs=[pl.BlockSpec(memory_space=pltpu.VMEM)] * len(counts),
        compiler_params=pltpu.CompilerParams(vmem_limit_bytes=24 * MIB),
        cost_estimate=pl.CostEstimate(flops=planes * 16 * N**3, bytes_accessed=planes * 8 * N * N, transcendentals=0),
        name="lateral",
    )(*ins, left, right)


def middle_kernel(sb, so, sa, mb, mo, ma, tf_ref, ta_ref, left_ref, right_ref, own, other, back):
    tf = tf_ref[...]
    ta = ta_ref[...]

    def smooth(a):
        return jnp.concatenate([r[pl.ds(a, r.shape[0] // PITCH, stride=PITCH), :] for r in (sb, so, sa)], 0)

    def recorded(a):
        return jnp.concatenate([r[a] for r in (mb, mo, ma)], 0)

    @pl.loop(0, N // STEP)
    def _(i):
        firsts = [STEP * i + j for j in range(0, STEP, 2)]
        blurred = [left_product(tf, jnp.concatenate([smooth(a), smooth(a + 1)], 1)) for a in firsts]
        ratios = []
        for a, blur in zip(firsts, blurred):
            rec = jnp.concatenate([recorded(a), recorded(a + 1)], 1)
            ratios.append(jnp.where(rec > 0, rec / blur, 0.0))
        for a, ratio in zip(firsts, ratios):
            res = left_product(ta, ratio)
            back[pl.ds(a, SLAB, stride=PITCH), :] = res[:, :N]
            back[pl.ds(a + 1, SLAB, stride=PITCH), :] = res[:, N:]

    left = left_ref[...]
    right = right_ref[...]

    @pl.loop(0, SLAB // STEP)
    def _(i):
        zs = [STEP * i + j for j in range(STEP)]
        logs = jnp.log(two_sided([back[pl.ds(z * PITCH, N), :] for z in zs], left, right))
        for j, z in enumerate(zs):
            for p in range(8):
                own[p, z] = logs[j * N + 8 * p : j * N + 8 * p + 8]
                other[p, z] = logs[j * N + 64 + 8 * p : j * N + 64 + 8 * p + 8]


def middle(smooth, recorded, tf, ta, left, right):
    ins = [*smooth, *recorded, tf, ta, left, right]
    half = jax.ShapeDtypeStruct((8, SLAB, 8, N), F32)
    return pl.pallas_call(
        middle_kernel,
        out_shape=[half, half],
        in_specs=[pl.BlockSpec(memory_space=pltpu.VMEM)] * len(ins),
        out_specs=[pl.BlockSpec(memory_space=pltpu.VMEM)] * 2,
        scratch_shapes=[pltpu.VMEM((SLAB * PITCH, N), F32)],
        compiler_params=pltpu.CompilerParams(vmem_limit_bytes=32 * MIB),
        cost_estimate=pl.CostEstimate(flops=8 * 10**9, bytes_accessed=15 * MIB, transcendentals=SLAB * N * N),
        name="middle",
    )(*ins)


def operand_rows(m):
    hi, lo = split(m)
    return jnp.concatenate([hi, lo], 0)


def twice(m, axis):
    return jnp.concatenate([m, m], axis)


def operand_cols(m):
    hi, lo = split(twice(m, 0))
    return jnp.concatenate([hi, lo], 1)


def prep_kernel(
    starts, taps, mx_ref, my_ref, rec,
    tf, ta, x_all, x_halves, x_pieces, adj_x, fwd_y, adj_y, rec_t, rec_first, rec_last, xt_ref,
):
    def toeplitz(rows, cols, flip):
        i = lax.broadcasted_iota(jnp.int32, (rows, 2 * cols), 0)
        j = lax.broadcasted_iota(jnp.int32, (rows, 2 * cols), 1)
        diag = jnp.where(j >= cols, j - cols, j) - i
        out = jnp.zeros((rows, 2 * cols), F32)
        for k in range(DEPTH):
            out = jnp.where(diag == k, taps[0, DEPTH - 1 - k if flip else k], out)
        return out

    tf[...] = operand_rows(toeplitz(SLAB + 2 * HALF, SLAB + 2 * FAR, False))
    ta[...] = operand_rows(toeplitz(SLAB, SLAB + 2 * HALF, True))
    mx = mx_ref[...]
    my = my_ref[...]
    x_all[...] = operand_rows(twice(mx, 1))
    fwd_y[...] = operand_cols(my.T)
    adj_y[...] = operand_cols(my)
    xt_ref[...] = mx.T

    def row_blocks(rows):
        return jnp.concatenate([xt_ref[pl.ds(pl.multiple_of(r, 8), 8), :] for r in rows], 0)

    pieces = row_blocks([starts[p] for p in range(16)])
    adj_x[...] = operand_rows(twice(pieces, 1))
    x_pieces[...] = operand_rows(twice(pieces.T, 1))
    core = starts[16]
    halves = row_blocks([core * 64 + 8 * p for p in range(8)] + [64 - core * 64 + 8 * p for p in range(8)])
    x_halves[...] = operand_rows(twice(halves.T, 1))

    @pl.loop(0, N // 8)
    def _(i):
        at = pl.multiple_of(8 * i, 8)
        for zb in range(0, SLAB, 8):
            block = jnp.stack([rec[z, pl.ds(at, 8), :] for z in range(zb, zb + 8)], 0)
            block = jnp.swapaxes(block, 0, 1)
            for j in range(8):
                rec_t[at + j, zb : zb + 8, :] = block[j]
                if zb < HALF:
                    rec_first[at + j, zb : zb + 8, :] = block[j]
                if zb >= SLAB - HALF:
                    rec_last[at + j, zb - SLAB + HALF : zb - SLAB + HALF + 8, :] = block[j]


def prep(starts, taps, mx, my, rec):
    full = SLAB + 2 * HALF
    wide = SLAB + 2 * FAR
    square = jax.ShapeDtypeStruct((2 * N, 2 * N), BF16)
    edge = jax.ShapeDtypeStruct((N, HALF, N), F32)
    outs = [
        jax.ShapeDtypeStruct((2 * full, 2 * wide), BF16),
        jax.ShapeDtypeStruct((2 * SLAB, 2 * full), BF16),
        *[square] * 6,
        jax.ShapeDtypeStruct((N, SLAB, N), F32),
        edge,
        edge,
    ]
    vmem = pl.BlockSpec(memory_space=pltpu.VMEM)
    smem = pl.BlockSpec(memory_space=pltpu.SMEM)
    return pl.pallas_call(
        prep_kernel,
        out_shape=outs,
        in_specs=[smem, smem, vmem, vmem, vmem],
        out_specs=[vmem] * len(outs),
        scratch_shapes=[pltpu.VMEM((N, N), F32)],
        compiler_params=pltpu.CompilerParams(vmem_limit_bytes=20 * MIB),
        name="prep",
    )(starts, taps, mx, my, rec)


def place_kernel(starts, *refs):
    out = refs[-1]
    at = 0
    for ref in refs[:-1]:
        for p in range(ref.shape[0]):
            begin = pl.multiple_of(starts[at], 8)
            out[:, pl.ds(begin, 8), :] = ref[p]
            at += 1


def place(starts, pieces):
    return pl.pallas_call(
        place_kernel,
        out_shape=jax.ShapeDtypeStruct((SLAB, N, N), F32),
        in_specs=[pl.BlockSpec(memory_space=pltpu.SMEM)] + [pl.BlockSpec(memory_space=pltpu.VMEM)] * len(pieces),
        out_specs=pl.BlockSpec(memory_space=pltpu.VMEM),
        compiler_params=pltpu.CompilerParams(vmem_limit_bytes=16 * MIB),
        name="place",
    )(starts, *pieces)


def to_core(x):
    return lax.ppermute(x, "view", [(i, i ^ 1) for i in range(8)])


def to_next(x):
    return lax.ppermute(x, "view", [(i, (i + 2) % 8) for i in range(8)])


def to_prev(x):
    return lax.ppermute(x, "view", [(i, (i - 2) % 8) for i in range(8)])


def up(x):
    n = lax.axis_size("gz")
    return lax.ppermute(x, "gz", [(i, i + 1) for i in range(n - 1)])


def down(x):
    n = lax.axis_size("gz")
    return lax.ppermute(x, "gz", [(i + 1, i) for i in range(n - 1)])


def reduce_chunk(other, own):
    total = own + to_core(other)
    from_prev = to_next(total[0:2])
    from_next = to_prev(total[2:4])
    from_prev, from_next = lax.optimization_barrier((from_prev, from_next))
    fwd_next = total[4:5] + from_prev[0:1]
    fwd_prev = total[5:6] + from_next[0:1]
    fwd_next, fwd_prev = lax.optimization_barrier((fwd_next, fwd_prev))
    last_a = to_next(fwd_next)
    last_b = to_prev(fwd_prev)
    last_a, last_b = lax.optimization_barrier((last_a, last_b))
    a = total[6:7] + from_next[1:2] + last_a
    b = total[7:8] + from_prev[1:2] + last_b
    return jnp.concatenate([a, b], 0)


def on_device(estimate, measured, lateral_x, lateral_y, depth_taps):
    view = lax.axis_index("view")
    core = lax.rem(view, 2)
    chip = lax.div(view, 2)
    recorded = measured[0]
    mx = lateral_x[0]
    my = lateral_y[0]

    nxt, prv, opp = (chip + 1) % 4, (chip + 3) % 4, (chip + 2) % 4
    order = jnp.stack([2 * opp, 2 * nxt + 1, 2 * opp + 1, 2 * prv, 2 * nxt, 2 * prv + 1, 2 * chip, 2 * chip + 1])
    starts = jnp.concatenate([core * 64 + 8 * order, (1 - core) * 64 + 8 * order, core[None]]).astype(jnp.int32)

    half = lax.dynamic_slice_in_dim(estimate, core * 64, 64, axis=1)
    before = up(half[SLAB - FAR :])
    after = down(half[:FAR])
    tf, ta, x_all, x_halves, x_fwd, adj_x, fwd_y, adj_y, rec_own, rec_first, rec_last = prep(
        starts, depth_taps, mx, my, recorded
    )
    before, after, rec_first, rec_last = lax.optimization_barrier((before, after, rec_first, rec_last))
    rec_before = up(rec_last)
    rec_after = down(rec_first)
    before2, after2 = to_core(before), to_core(after)

    def middle_of(smooth):
        return middle(smooth, (rec_before, rec_own, rec_after), tf, ta, adj_x, adj_y)

    mine = jnp.stack(
        [lax.dynamic_slice_in_dim(estimate, starts[6 + k], 8, axis=1) for k in range(2)], 0
    )

    (smooth_own,) = lateral([[estimate]], x_all, fwd_y)
    smooth_b, smooth_a = lateral([[before, before2], [after, after2]], x_halves, fwd_y)
    own, other = middle_of((smooth_b, smooth_own, smooth_a))
    mine = mine * jnp.exp(reduce_chunk(other, own) / 8.0)

    prev_c, next_c = to_next(mine), to_prev(mine)
    b0, a0 = up(mine[:, SLAB - FAR :]), down(mine[:, :FAR])
    opp_a, opp_b = to_next(prev_c[0:1]), to_prev(next_c[1:2])
    sides = jnp.concatenate([prev_c, next_c], 0)
    b1, a1 = up(sides[:, SLAB - FAR :]), down(sides[:, :FAR])
    near = jnp.concatenate([mine, sides], 0)
    near2 = to_core(near)
    opp_c = jnp.concatenate([opp_a, opp_b], 0)
    b2, a2 = up(opp_c[:, SLAB - FAR :]), down(opp_c[:, :FAR])
    opp2 = to_core(opp_c)
    ends = jnp.concatenate([b0, b1, a0, a1], 0)
    ends2 = to_core(ends)
    tail = jnp.concatenate([b2, a2], 0)
    tail2 = to_core(tail)

    def in_order(near, opp_c):
        mine, prv, nxt = near[0:2], near[2:4], near[4:6]
        return [opp_c[0:1], nxt[1:2], opp_c[1:2], prv[0:1], nxt[0:1], prv[1:2], mine]

    (smooth_own,) = lateral([in_order(near, opp_c) + in_order(near2, opp2)], x_fwd, fwd_y)
    smooth_b, smooth_a = lateral(
        [
            in_order(ends[0:6], tail[0:2]) + in_order(ends2[0:6], tail2[0:2]),
            in_order(ends[6:12], tail[2:4]) + in_order(ends2[6:12], tail2[2:4]),
        ],
        x_fwd,
        fwd_y,
    )
    own, other = middle_of((smooth_b, smooth_own, smooth_a))
    mine = mine * jnp.exp(reduce_chunk(other, own) / 8.0)
    prev_c, next_c = to_next(mine), to_prev(mine)
    near = jnp.concatenate([mine, prev_c, next_c], 0)
    near2 = to_core(near)
    opp_c = jnp.concatenate([to_next(prev_c[0:1]), to_prev(next_c[1:2])], 0)
    opp2 = to_core(opp_c)
    return place(starts, in_order(near, opp_c) + in_order(near2, opp2))


def solution(mesh):
    return jax.shard_map(
        on_device,
        mesh=mesh,
        in_specs=(
            P("gz", None, None),
            P("view", "gz", None, None),
            P("view", None, None),
            P("view", None, None),
            P("view", None),
        ),
        out_specs=P("gz", None, None),
        check_vma=False,
    )
```

```python
import jax
import jax.numpy as jnp
from jax import lax
from jax.experimental import pallas as pl
from jax.experimental.pallas import tpu as pltpu
from jax.sharding import PartitionSpec as P

DEPTH = 33
HALF = 16
N = 128
SLAB = 48
FAR = 2 * HALF
F32 = jnp.float32
BF16 = jnp.bfloat16
MIB = 1024 * 1024
PITCH = 132
STEP = 16


def split(x):
    hi = x.astype(BF16)
    return hi, (x - hi.astype(F32)).astype(BF16)


def left_product(operand, x):
    hi, lo = split(x)
    out = jnp.dot(operand, jnp.concatenate([hi, lo], 0), preferred_element_type=F32)
    rows = operand.shape[0] // 2
    return out[:rows] + out[rows:]


def right_product(x, operand):
    hi, lo = split(x)
    out = jnp.dot(jnp.concatenate([hi, lo], 1), operand, preferred_element_type=F32)
    cols = operand.shape[1] // 2
    return out[:, :cols] + out[:, cols:]


def two_sided(planes, left, right):
    sides = [
        left_product(left, jnp.concatenate(planes[i : i + 2], 1)) for i in range(0, len(planes), 2)
    ]
    rows = jnp.concatenate([part for s in sides for part in (s[:, :N], s[:, N:])], 0)
    return right_product(rows, right)


def region_plane(refs, z):
    blocks = []
    for ref in refs:
        if len(ref.shape) == 3:
            blocks.append(ref[z])
        else:
            blocks.extend(ref[p, z] for p in range(ref.shape[0]))
    return jnp.concatenate(blocks, 0) if len(blocks) > 1 else blocks[0]


def lateral_kernel(counts, *refs):
    total = sum(c for c, _ in counts)
    ins, (left_ref, right_ref), outs = refs[:total], refs[total : total + 2], refs[total + 2 :]
    left = left_ref[...]
    right = right_ref[...]
    at = 0
    for (count, planes), out in zip(counts, outs):
        region = ins[at : at + count]
        at += count

        @pl.loop(0, planes // STEP)
        def _(i, region=region, out=out):
            zs = [STEP * i + j for j in range(STEP)]
            res = two_sided([region_plane(region, z) for z in zs], left, right)
            for j, z in enumerate(zs):
                out[pl.ds(z * PITCH, N), :] = res[j * N : j * N + N]


def lateral(regions, left, right):
    counts = []
    ins = []
    for region in regions:
        ref = region[0]
        counts.append((len(region), ref.shape[0] if ref.ndim == 3 else ref.shape[1]))
        ins.extend(region)
    planes = sum(p for _, p in counts)
    return pl.pallas_call(
        lambda *refs: lateral_kernel(counts, *refs),
        out_shape=[jax.ShapeDtypeStruct((p * PITCH, N), F32) for _, p in counts],
        in_specs=[pl.BlockSpec(memory_space=pltpu.VMEM)] * (len(ins) + 2),
        out_specs=[pl.BlockSpec(memory_space=pltpu.VMEM)] * len(counts),
        compiler_params=pltpu.CompilerParams(vmem_limit_bytes=24 * MIB),
        cost_estimate=pl.CostEstimate(flops=planes * 16 * N**3, bytes_accessed=planes * 8 * N * N, transcendentals=0),
        name="lateral",
    )(*ins, left, right)


def strided(refs, a):
    return jnp.concatenate([r[pl.ds(a, r.shape[0] // PITCH, stride=PITCH), :] for r in refs], 0)


def at_row(refs, a):
    return jnp.concatenate([r[a] for r in refs], 0)


def pair(pick, refs, a):
    return jnp.concatenate([pick(refs, a), pick(refs, a + 1)], 1)


def store_back(back, a, res):
    back[pl.ds(a, SLAB, stride=PITCH), :] = res[:, :N]
    back[pl.ds(a + 1, SLAB, stride=PITCH), :] = res[:, N:]


def logs_out(back, left_ref, right_ref, own, other):
    left = left_ref[...]
    right = right_ref[...]

    @pl.loop(0, SLAB // STEP)
    def _(i):
        zs = [STEP * i + j for j in range(STEP)]
        logs = jnp.log(two_sided([back[pl.ds(z * PITCH, N), :] for z in zs], left, right))
        for j, z in enumerate(zs):
            for p in range(8):
                own[p, z] = logs[j * N + 8 * p : j * N + 8 * p + 8]
                other[p, z] = logs[j * N + 64 + 8 * p : j * N + 64 + 8 * p + 8]


def ratio_kernel(sb, so, sa, rec, tf_ref, out, first, last):
    tf = tf_ref[...]

    @pl.loop(0, N // STEP)
    def _(i):
        firsts = [STEP * i + j for j in range(0, STEP, 2)]
        blurred = [left_product(tf, pair(strided, (sb, so, sa), a)) for a in firsts]
        for a, blur in zip(firsts, blurred):
            both = pair(at_row, (rec,), a) / blur
            for k in range(2):
                ratio = both[:, k * N : k * N + N]
                out[a + k] = ratio
                first[a + k] = ratio[:HALF]
                last[a + k] = ratio[SLAB - HALF :]


def adjoint_kernel(rb, ro, ra, ta_ref, left_ref, right_ref, own, other, back):
    ta = ta_ref[...]

    @pl.loop(0, N // STEP)
    def _(i):
        for a in [STEP * i + j for j in range(0, STEP, 2)]:
            store_back(back, a, left_product(ta, pair(at_row, (rb, ro, ra), a)))

    logs_out(back, left_ref, right_ref, own, other)


def middle_kernel(sb, so, sa, mb, mo, ma, tf_ref, ta_ref, left_ref, right_ref, own, other, back):
    tf = tf_ref[...]
    ta = ta_ref[...]

    @pl.loop(0, N // STEP)
    def _(i):
        firsts = [STEP * i + j for j in range(0, STEP, 2)]
        blurred = [left_product(tf, pair(strided, (sb, so, sa), a)) for a in firsts]
        ratios = []
        for a, blur in zip(firsts, blurred):
            rec = pair(at_row, (mb, mo, ma), a)
            ratios.append(jnp.where(rec > 0, rec / blur, 0.0))
        for a, ratio in zip(firsts, ratios):
            store_back(back, a, left_product(ta, ratio))

    logs_out(back, left_ref, right_ref, own, other)


def kernel_call(kernel, ins, outs, scratch, flops, name):
    return pl.pallas_call(
        kernel,
        out_shape=outs,
        in_specs=[pl.BlockSpec(memory_space=pltpu.VMEM)] * len(ins),
        out_specs=[pl.BlockSpec(memory_space=pltpu.VMEM)] * len(outs),
        scratch_shapes=scratch,
        compiler_params=pltpu.CompilerParams(vmem_limit_bytes=32 * MIB),
        cost_estimate=pl.CostEstimate(flops=flops, bytes_accessed=15 * MIB, transcendentals=SLAB * N * N),
        name=name,
    )(*ins)


def ratio_of(smooth, recorded, tf):
    edge = jax.ShapeDtypeStruct((N, HALF, N), F32)
    outs = [jax.ShapeDtypeStruct((N, SLAB, N), F32), edge, edge]
    return kernel_call(ratio_kernel, (*smooth, recorded, tf), outs, [], 3 * 10**9, "ratio")


def adjoint(ratios, ta, left, right):
    half = jax.ShapeDtypeStruct((8, SLAB, 8, N), F32)
    back = [pltpu.VMEM((SLAB * PITCH, N), F32)]
    return kernel_call(adjoint_kernel, (*ratios, ta, left, right), [half, half], back, 5 * 10**9, "adjoint")


def middle(smooth, recorded, tf, ta, left, right):
    half = jax.ShapeDtypeStruct((8, SLAB, 8, N), F32)
    back = [pltpu.VMEM((SLAB * PITCH, N), F32)]
    return kernel_call(middle_kernel, (*smooth, *recorded, tf, ta, left, right), [half, half], back, 8 * 10**9, "middle")


def operand_rows(m):
    hi, lo = split(m)
    return jnp.concatenate([hi, lo], 0)


def twice(m, axis):
    return jnp.concatenate([m, m], axis)


def operand_cols(m):
    hi, lo = split(twice(m, 0))
    return jnp.concatenate([hi, lo], 1)


def prep_kernel(
    starts, taps, mx_ref, my_ref, rec,
    tf, ts, ta, x_all, x_halves, x_pieces, adj_x, fwd_y, adj_y, rec_t, rec_first, rec_last, xt_ref,
):
    def toeplitz(rows, cols, flip):
        i = lax.broadcasted_iota(jnp.int32, (rows, 2 * cols), 0)
        j = lax.broadcasted_iota(jnp.int32, (rows, 2 * cols), 1)
        diag = jnp.where(j >= cols, j - cols, j) - i
        out = jnp.zeros((rows, 2 * cols), F32)
        for k in range(DEPTH):
            out = jnp.where(diag == k, taps[0, DEPTH - 1 - k if flip else k], out)
        return out

    tf[...] = operand_rows(toeplitz(SLAB + 2 * HALF, SLAB + 2 * FAR, False))
    ts[...] = operand_rows(toeplitz(SLAB, SLAB + 2 * HALF, False))
    ta[...] = operand_rows(toeplitz(SLAB, SLAB + 2 * HALF, True))
    mx = mx_ref[...]
    my = my_ref[...]
    x_all[...] = operand_rows(twice(mx, 1))
    fwd_y[...] = operand_cols(my.T)
    adj_y[...] = operand_cols(my)
    xt_ref[...] = mx.T

    def row_blocks(rows):
        return jnp.concatenate([xt_ref[pl.ds(pl.multiple_of(r, 8), 8), :] for r in rows], 0)

    pieces = row_blocks([starts[p] for p in range(16)])
    adj_x[...] = operand_rows(twice(pieces, 1))
    x_pieces[...] = operand_rows(twice(pieces.T, 1))
    core = starts[16]
    halves = row_blocks([core * 64 + 8 * p for p in range(8)] + [64 - core * 64 + 8 * p for p in range(8)])
    x_halves[...] = operand_rows(twice(halves.T, 1))

    @pl.loop(0, N // 8)
    def _(i):
        at = pl.multiple_of(8 * i, 8)
        for zb in range(0, SLAB, 8):
            block = jnp.stack([rec[z, pl.ds(at, 8), :] for z in range(zb, zb + 8)], 0)
            block = jnp.swapaxes(block, 0, 1)
            for j in range(8):
                rec_t[at + j, zb : zb + 8, :] = block[j]
                if zb < HALF:
                    rec_first[at + j, zb : zb + 8, :] = block[j]
                if zb >= SLAB - HALF:
                    rec_last[at + j, zb - SLAB + HALF : zb - SLAB + HALF + 8, :] = block[j]


def prep(starts, taps, mx, my, rec):
    full = SLAB + 2 * HALF
    wide = SLAB + 2 * FAR
    square = jax.ShapeDtypeStruct((2 * N, 2 * N), BF16)
    edge = jax.ShapeDtypeStruct((N, HALF, N), F32)
    outs = [
        jax.ShapeDtypeStruct((2 * full, 2 * wide), BF16),
        jax.ShapeDtypeStruct((2 * SLAB, 2 * full), BF16),
        jax.ShapeDtypeStruct((2 * SLAB, 2 * full), BF16),
        *[square] * 6,
        jax.ShapeDtypeStruct((N, SLAB, N), F32),
        edge,
        edge,
    ]
    vmem = pl.BlockSpec(memory_space=pltpu.VMEM)
    smem = pl.BlockSpec(memory_space=pltpu.SMEM)
    return pl.pallas_call(
        prep_kernel,
        out_shape=outs,
        in_specs=[smem, smem, vmem, vmem, vmem],
        out_specs=[vmem] * len(outs),
        scratch_shapes=[pltpu.VMEM((N, N), F32)],
        compiler_params=pltpu.CompilerParams(vmem_limit_bytes=20 * MIB),
        name="prep",
    )(starts, taps, mx, my, rec)


def place_kernel(starts, *refs):
    out = refs[-1]
    at = 0
    for ref in refs[:-1]:
        for p in range(ref.shape[0]):
            begin = pl.multiple_of(starts[at], 8)
            out[:, pl.ds(begin, 8), :] = ref[p]
            at += 1


def place(starts, pieces):
    return pl.pallas_call(
        place_kernel,
        out_shape=jax.ShapeDtypeStruct((SLAB, N, N), F32),
        in_specs=[pl.BlockSpec(memory_space=pltpu.SMEM)] + [pl.BlockSpec(memory_space=pltpu.VMEM)] * len(pieces),
        out_specs=pl.BlockSpec(memory_space=pltpu.VMEM),
        compiler_params=pltpu.CompilerParams(vmem_limit_bytes=16 * MIB),
        name="place",
    )(starts, *pieces)


def to_core(x):
    return lax.ppermute(x, "view", [(i, i ^ 1) for i in range(8)])


def to_next(x):
    return lax.ppermute(x, "view", [(i, (i + 2) % 8) for i in range(8)])


def to_prev(x):
    return lax.ppermute(x, "view", [(i, (i - 2) % 8) for i in range(8)])


def up(x):
    n = lax.axis_size("gz")
    return lax.ppermute(x, "gz", [(i, i + 1) for i in range(n - 1)])


def down(x):
    n = lax.axis_size("gz")
    return lax.ppermute(x, "gz", [(i + 1, i) for i in range(n - 1)])


def reduce_chunk(other, own, beside=None):
    total = own + to_core(other)
    from_prev = to_next(total[0:2])
    from_next = to_prev(total[2:4])
    extra = beside(total) if beside else ()
    from_prev, from_next = lax.optimization_barrier((from_prev, from_next))
    fwd_next = total[4:5] + from_prev[0:1]
    fwd_prev = total[5:6] + from_next[0:1]
    fwd_next, fwd_prev = lax.optimization_barrier((fwd_next, fwd_prev))
    last_a = to_next(fwd_next)
    last_b = to_prev(fwd_prev)
    last_a, last_b, *extra = lax.optimization_barrier((last_a, last_b, *extra))
    a = total[6:7] + from_next[1:2] + last_a
    b = total[7:8] + from_prev[1:2] + last_b
    return jnp.concatenate([a, b], 0), extra


def on_device(estimate, measured, lateral_x, lateral_y, depth_taps):
    view = lax.axis_index("view")
    core = lax.rem(view, 2)
    chip = lax.div(view, 2)
    recorded = measured[0]
    mx = lateral_x[0]
    my = lateral_y[0]

    nxt, prv, opp = (chip + 1) % 4, (chip + 3) % 4, (chip + 2) % 4
    order = jnp.stack([2 * opp, 2 * nxt + 1, 2 * opp + 1, 2 * prv, 2 * nxt, 2 * prv + 1, 2 * chip, 2 * chip + 1])
    starts = jnp.concatenate([core * 64 + 8 * order, (1 - core) * 64 + 8 * order, core[None]]).astype(jnp.int32)

    before = up(lax.dynamic_slice(estimate, (SLAB - HALF, core * 64, 0), (HALF, 64, N)))
    after = down(lax.dynamic_slice(estimate, (0, core * 64, 0), (HALF, 64, N)))
    tf, ts, ta, x_all, x_halves, x_fwd, adj_x, fwd_y, adj_y, rec_own, rec_first, rec_last = prep(
        starts, depth_taps, mx, my, recorded
    )
    (smooth_own,) = lateral([[estimate]], x_all, fwd_y)
    before, after = lax.optimization_barrier((before, after))
    before2, after2 = to_core(before), to_core(after)
    smooth_b, smooth_a = lateral([[before, before2], [after, after2]], x_halves, fwd_y)
    ratio, ratio_first, ratio_last = ratio_of((smooth_b, smooth_own, smooth_a), rec_own, ts)
    ratio_b = up(ratio_last)
    ratio_a = down(ratio_first)
    mine = jnp.stack([lax.dynamic_slice_in_dim(estimate, starts[6 + k], 8, axis=1) for k in range(2)], 0)
    own, other = adjoint((ratio_b, ratio, ratio_a), ta, adj_x, adj_y)

    def recorded_halo(total):
        last, first, _ = lax.optimization_barrier((rec_last, rec_first, total))
        return up(last), down(first)

    log_sum, (rec_before, rec_after) = reduce_chunk(other, own, recorded_halo)
    mine = mine * jnp.exp(log_sum / 8.0)

    prev_c, next_c = to_next(mine), to_prev(mine)
    b0, a0 = up(mine[:, SLAB - FAR :]), down(mine[:, :FAR])
    prev_c, next_c, b0, a0 = lax.optimization_barrier((prev_c, next_c, b0, a0))
    opp_a, opp_b = to_next(prev_c[0:1]), to_prev(next_c[1:2])
    sides = jnp.concatenate([prev_c, next_c], 0)
    b1, a1 = up(sides[:, SLAB - FAR :]), down(sides[:, :FAR])
    near = jnp.concatenate([mine, sides], 0)
    near2 = to_core(near)
    opp_a, opp_b, near2 = lax.optimization_barrier((opp_a, opp_b, near2))
    opp_c = jnp.concatenate([opp_a, opp_b], 0)
    b2, a2 = up(opp_c[:, SLAB - FAR :]), down(opp_c[:, :FAR])
    opp2 = to_core(opp_c)
    ends = jnp.concatenate([b0, b1, a0, a1], 0)
    ends2 = to_core(ends)
    tail = jnp.concatenate([b2, a2], 0)
    tail2 = to_core(tail)

    def in_order(near, opp_c):
        mine, prv, nxt = near[0:2], near[2:4], near[4:6]
        return [opp_c[0:1], nxt[1:2], opp_c[1:2], prv[0:1], nxt[0:1], prv[1:2], mine]

    (smooth_own,) = lateral([in_order(near, opp_c) + in_order(near2, opp2)], x_fwd, fwd_y)
    smooth_b, smooth_a = lateral(
        [
            in_order(ends[0:6], tail[0:2]) + in_order(ends2[0:6], tail2[0:2]),
            in_order(ends[6:12], tail[2:4]) + in_order(ends2[6:12], tail2[2:4]),
        ],
        x_fwd,
        fwd_y,
    )
    smooth = (smooth_b, smooth_own, smooth_a)
    own, other = middle(smooth, (rec_before, rec_own, rec_after), tf, ta, adj_x, adj_y)
    log_sum, _ = reduce_chunk(other, own)
    mine = mine * jnp.exp(log_sum / 8.0)
    prev_c, next_c = lax.optimization_barrier((to_next(mine), to_prev(mine)))
    near = jnp.concatenate([mine, prev_c, next_c], 0)
    near2 = to_core(near)
    opp_c = jnp.concatenate([to_next(prev_c[0:1]), to_prev(next_c[1:2])], 0)
    opp2 = to_core(opp_c)
    return place(starts, in_order(near, opp_c) + in_order(near2, opp2))


def solution(mesh):
    return jax.shard_map(
        on_device,
        mesh=mesh,
        in_specs=(
            P("gz", None, None),
            P("view", "gz", None, None),
            P("view", None, None),
            P("view", None, None),
            P("view", None),
        ),
        out_specs=P("gz", None, None),
        check_vma=False,
    )
```

```python
import jax
import jax.numpy as jnp
from jax import lax
from jax.experimental import pallas as pl
from jax.experimental.pallas import tpu as pltpu
from jax.sharding import PartitionSpec as P

DEPTH = 33
HALF = 16
N = 128
SLAB = 48
FAR = 2 * HALF
F32 = jnp.float32
BF16 = jnp.bfloat16
MIB = 1024 * 1024
PITCH = 132
STEP = 16


def split(x):
    hi = x.astype(BF16)
    return hi, (x - hi.astype(F32)).astype(BF16)


def left_product(operand, x):
    hi, lo = split(x)
    out = jnp.dot(operand, jnp.concatenate([hi, lo], 0), preferred_element_type=F32)
    rows = operand.shape[0] // 2
    return out[:rows] + out[rows:]


def right_product(x, operand):
    hi, lo = split(x)
    out = jnp.dot(jnp.concatenate([hi, lo], 1), operand, preferred_element_type=F32)
    cols = operand.shape[1] // 2
    return out[:, :cols] + out[:, cols:]


def two_sided(planes, left, right):
    sides = [
        left_product(left, jnp.concatenate(planes[i : i + 2], 1)) for i in range(0, len(planes), 2)
    ]
    rows = jnp.concatenate([part for s in sides for part in (s[:, :N], s[:, N:])], 0)
    return right_product(rows, right)


def region_plane(refs, z):
    blocks = []
    for ref in refs:
        if len(ref.shape) == 3:
            blocks.append(ref[z])
        else:
            blocks.extend(ref[p, z] for p in range(ref.shape[0]))
    return jnp.concatenate(blocks, 0) if len(blocks) > 1 else blocks[0]


def lateral_kernel(counts, *refs):
    total = sum(c for c, _ in counts)
    ins, (left_ref, right_ref), outs = refs[:total], refs[total : total + 2], refs[total + 2 :]
    left = left_ref[...]
    right = right_ref[...]
    at = 0
    for (count, planes), out in zip(counts, outs):
        region = ins[at : at + count]
        at += count

        @pl.loop(0, planes // STEP)
        def _(i, region=region, out=out):
            zs = [STEP * i + j for j in range(STEP)]
            res = two_sided([region_plane(region, z) for z in zs], left, right)
            for j, z in enumerate(zs):
                out[pl.ds(z * PITCH, N), :] = res[j * N : j * N + N]


def lateral(regions, left, right):
    counts = []
    ins = []
    for region in regions:
        ref = region[0]
        counts.append((len(region), ref.shape[0] if ref.ndim == 3 else ref.shape[1]))
        ins.extend(region)
    planes = sum(p for _, p in counts)
    return pl.pallas_call(
        lambda *refs: lateral_kernel(counts, *refs),
        out_shape=[jax.ShapeDtypeStruct((p * PITCH, N), F32) for _, p in counts],
        in_specs=[pl.BlockSpec(memory_space=pltpu.VMEM)] * (len(ins) + 2),
        out_specs=[pl.BlockSpec(memory_space=pltpu.VMEM)] * len(counts),
        compiler_params=pltpu.CompilerParams(vmem_limit_bytes=8 * MIB),
        cost_estimate=pl.CostEstimate(flops=planes * 16 * N**3, bytes_accessed=planes * 8 * N * N, transcendentals=0),
        name="lateral",
    )(*ins, left, right)


def strided(refs, a):
    return jnp.concatenate([r[pl.ds(a, r.shape[0] // PITCH, stride=PITCH), :] for r in refs], 0)


def at_row(refs, a):
    return jnp.concatenate([r[a] for r in refs], 0)


def pair(pick, refs, a):
    return jnp.concatenate([pick(refs, a), pick(refs, a + 1)], 1)


def store_back(back, a, res):
    back[pl.ds(a, SLAB, stride=PITCH), :] = res[:, :N]
    back[pl.ds(a + 1, SLAB, stride=PITCH), :] = res[:, N:]


def logs_out(back, left_ref, right_ref, own, other):
    left = left_ref[...]
    right = right_ref[...]

    @pl.loop(0, SLAB // STEP)
    def _(i):
        zs = [STEP * i + j for j in range(STEP)]
        logs = jnp.log(two_sided([back[pl.ds(z * PITCH, N), :] for z in zs], left, right))
        for j, z in enumerate(zs):
            for p in range(8):
                own[p, z] = logs[j * N + 8 * p : j * N + 8 * p + 8]
                other[p, z] = logs[j * N + 64 + 8 * p : j * N + 64 + 8 * p + 8]


def middle_kernel(sb, so, sa, mb, mo, ma, tf_ref, ta_ref, left_ref, right_ref, own, other, back):
    tf = tf_ref[...]
    ta = ta_ref[...]

    @pl.loop(0, N // STEP)
    def _(i):
        firsts = [STEP * i + j for j in range(0, STEP, 2)]
        blurred = [left_product(tf, pair(strided, (sb, so, sa), a)) for a in firsts]
        ratios = []
        for a, blur in zip(firsts, blurred):
            rec = pair(at_row, (mb, mo, ma), a)
            ratios.append(jnp.where(rec > 0, rec / blur, 0.0))
        for a, ratio in zip(firsts, ratios):
            store_back(back, a, left_product(ta, ratio))

    logs_out(back, left_ref, right_ref, own, other)


def middle(smooth, recorded, tf, ta, left, right):
    ins = (*smooth, *recorded, tf, ta, left, right)
    half = jax.ShapeDtypeStruct((8, SLAB, 8, N), F32)
    return pl.pallas_call(
        middle_kernel,
        out_shape=[half, half],
        in_specs=[pl.BlockSpec(memory_space=pltpu.VMEM)] * len(ins),
        out_specs=[pl.BlockSpec(memory_space=pltpu.VMEM)] * 2,
        scratch_shapes=[pltpu.VMEM((SLAB * PITCH, N), F32)],
        compiler_params=pltpu.CompilerParams(vmem_limit_bytes=12 * MIB),
        cost_estimate=pl.CostEstimate(flops=8 * 10**9, bytes_accessed=15 * MIB, transcendentals=SLAB * N * N),
        name="middle",
    )(*ins)


def operand_rows(m):
    hi, lo = split(m)
    return jnp.concatenate([hi, lo], 0)


def twice(m, axis):
    return jnp.concatenate([m, m], axis)


def operand_cols(m):
    hi, lo = split(twice(m, 0))
    return jnp.concatenate([hi, lo], 1)


def turn(src, dst):
    @pl.loop(0, N // 8)
    def _(i):
        at = pl.multiple_of(8 * i, 8)
        for zb in range(0, src.shape[0], 8):
            block = jnp.stack([src[z, pl.ds(at, 8), :] for z in range(zb, zb + 8)], 0)
            block = jnp.swapaxes(block, 0, 1)
            for j in range(8):
                dst[at + j, zb : zb + 8, :] = block[j]


def turn_kernel(before, after, before_t, after_t):
    turn(before, before_t)
    turn(after, after_t)


def turned(before, after):
    vmem = pl.BlockSpec(memory_space=pltpu.VMEM)
    edge = jax.ShapeDtypeStruct((N, HALF, N), F32)
    return pl.pallas_call(
        turn_kernel,
        out_shape=[edge, edge],
        in_specs=[vmem, vmem],
        out_specs=[vmem, vmem],
        compiler_params=pltpu.CompilerParams(vmem_limit_bytes=4 * MIB),
        name="turn",
    )(before, after)


def prep_kernel(
    starts, taps, mx_ref, my_ref, rec,
    tf, ta, x_all, x_halves, x_pieces, adj_x, fwd_y, adj_y, rec_t, xt_ref,
):
    def toeplitz(rows, cols, flip):
        i = lax.broadcasted_iota(jnp.int32, (rows, 2 * cols), 0)
        j = lax.broadcasted_iota(jnp.int32, (rows, 2 * cols), 1)
        diag = jnp.where(j >= cols, j - cols, j) - i
        out = jnp.zeros((rows, 2 * cols), F32)
        for k in range(DEPTH):
            out = jnp.where(diag == k, taps[0, DEPTH - 1 - k if flip else k], out)
        return out

    tf[...] = operand_rows(toeplitz(SLAB + 2 * HALF, SLAB + 2 * FAR, False))
    ta[...] = operand_rows(toeplitz(SLAB, SLAB + 2 * HALF, True))
    mx = mx_ref[...]
    my = my_ref[...]
    x_all[...] = operand_rows(twice(mx, 1))
    fwd_y[...] = operand_cols(my.T)
    adj_y[...] = operand_cols(my)
    xt_ref[...] = mx.T

    def row_blocks(rows):
        return jnp.concatenate([xt_ref[pl.ds(pl.multiple_of(r, 8), 8), :] for r in rows], 0)

    pieces = row_blocks([starts[p] for p in range(16)])
    adj_x[...] = operand_rows(twice(pieces, 1))
    x_pieces[...] = operand_rows(twice(pieces.T, 1))
    core = starts[16]
    halves = row_blocks([core * 64 + 8 * p for p in range(8)] + [64 - core * 64 + 8 * p for p in range(8)])
    x_halves[...] = operand_rows(twice(halves.T, 1))

    turn(rec, rec_t)


def prep(starts, taps, mx, my, rec):
    full = SLAB + 2 * HALF
    wide = SLAB + 2 * FAR
    square = jax.ShapeDtypeStruct((2 * N, 2 * N), BF16)
    outs = [
        jax.ShapeDtypeStruct((2 * full, 2 * wide), BF16),
        jax.ShapeDtypeStruct((2 * SLAB, 2 * full), BF16),
        *[square] * 6,
        jax.ShapeDtypeStruct((N, SLAB, N), F32),
    ]
    vmem = pl.BlockSpec(memory_space=pltpu.VMEM)
    smem = pl.BlockSpec(memory_space=pltpu.SMEM)
    return pl.pallas_call(
        prep_kernel,
        out_shape=outs,
        in_specs=[smem, smem, vmem, vmem, vmem],
        out_specs=[vmem] * len(outs),
        scratch_shapes=[pltpu.VMEM((N, N), F32)],
        compiler_params=pltpu.CompilerParams(vmem_limit_bytes=8 * MIB),
        name="prep",
    )(starts, taps, mx, my, rec)


def place_kernel(starts, *refs):
    out = refs[-1]
    at = 0
    for ref in refs[:-1]:
        for p in range(ref.shape[0]):
            begin = pl.multiple_of(starts[at], 8)
            out[:, pl.ds(begin, 8), :] = ref[p]
            at += 1


def place(starts, pieces):
    return pl.pallas_call(
        place_kernel,
        out_shape=jax.ShapeDtypeStruct((SLAB, N, N), F32),
        in_specs=[pl.BlockSpec(memory_space=pltpu.SMEM)] + [pl.BlockSpec(memory_space=pltpu.VMEM)] * len(pieces),
        out_specs=pl.BlockSpec(memory_space=pltpu.VMEM),
        compiler_params=pltpu.CompilerParams(vmem_limit_bytes=4 * MIB),
        name="place",
    )(starts, *pieces)


def to_core(x):
    return lax.ppermute(x, "view", [(i, i ^ 1) for i in range(8)])


def to_next(x):
    return lax.ppermute(x, "view", [(i, (i + 2) % 8) for i in range(8)])


def to_prev(x):
    return lax.ppermute(x, "view", [(i, (i - 2) % 8) for i in range(8)])


def up(x):
    n = lax.axis_size("gz")
    return lax.ppermute(x, "gz", [(i, i + 1) for i in range(n - 1)])


def down(x):
    n = lax.axis_size("gz")
    return lax.ppermute(x, "gz", [(i + 1, i) for i in range(n - 1)])


def reduce_chunk(other, own):
    total = own + to_core(other)
    from_prev = to_next(total[0:2])
    from_next = to_prev(total[2:4])
    from_prev, from_next = lax.optimization_barrier((from_prev, from_next))
    fwd_next = total[4:5] + from_prev[0:1]
    fwd_prev = total[5:6] + from_next[0:1]
    fwd_next, fwd_prev = lax.optimization_barrier((fwd_next, fwd_prev))
    last_a = to_next(fwd_next)
    last_b = to_prev(fwd_prev)
    last_a, last_b = lax.optimization_barrier((last_a, last_b))
    a = total[6:7] + from_next[1:2] + last_a
    b = total[7:8] + from_prev[1:2] + last_b
    return jnp.concatenate([a, b], 0)


def on_device(estimate, measured, lateral_x, lateral_y, depth_taps):
    view = lax.axis_index("view")
    core = lax.rem(view, 2)
    chip = lax.div(view, 2)
    recorded = measured[0]
    mx = lateral_x[0]
    my = lateral_y[0]

    nxt, prv, opp = (chip + 1) % 4, (chip + 3) % 4, (chip + 2) % 4
    order = jnp.stack([2 * opp, 2 * nxt + 1, 2 * opp + 1, 2 * prv, 2 * nxt, 2 * prv + 1, 2 * chip, 2 * chip + 1])
    starts = jnp.concatenate([core * 64 + 8 * order, (1 - core) * 64 + 8 * order, core[None]]).astype(jnp.int32)

    before = up(lax.dynamic_slice(estimate, (SLAB - FAR, core * 64, 0), (FAR, 64, N)))
    after = down(lax.dynamic_slice(estimate, (0, core * 64, 0), (FAR, 64, N)))
    rec_before = up(recorded[SLAB - HALF :])
    rec_after = down(recorded[:HALF])
    tf, ta, x_all, x_halves, x_fwd, adj_x, fwd_y, adj_y, rec_own = prep(starts, depth_taps, mx, my, recorded)
    mine = lax.dynamic_slice(estimate, (0, core * 64 + chip * 16, 0), (SLAB, 16, N))
    mine = jnp.stack([mine[:, :8], mine[:, 8:]], 0)
    before2, after2 = to_core(before), to_core(after)

    (smooth_own,) = lateral([[estimate]], x_all, fwd_y)
    smooth_b, smooth_a = lateral([[before, before2], [after, after2]], x_halves, fwd_y)
    rec_before, rec_after, smooth_b, smooth_a = lax.optimization_barrier((rec_before, rec_after, smooth_b, smooth_a))
    smooth = (smooth_b, smooth_own, smooth_a)
    rec_before, rec_after = turned(rec_before, rec_after)
    own, other = middle(smooth, (rec_before, rec_own, rec_after), tf, ta, adj_x, adj_y)
    mine = mine * jnp.exp(reduce_chunk(other, own) / 8.0)

    prev_c, next_c = to_next(mine), to_prev(mine)
    b0, a0 = up(mine[:, SLAB - FAR :]), down(mine[:, :FAR])
    prev_c, next_c, b0, a0 = lax.optimization_barrier((prev_c, next_c, b0, a0))
    opp_a, opp_b = to_next(prev_c[0:1]), to_prev(next_c[1:2])
    sides = jnp.concatenate([prev_c, next_c], 0)
    b1, a1 = up(sides[:, SLAB - FAR :]), down(sides[:, :FAR])
    near = jnp.concatenate([mine, sides], 0)
    near2 = to_core(near)
    opp_a, opp_b, near2 = lax.optimization_barrier((opp_a, opp_b, near2))
    opp_c = jnp.concatenate([opp_a, opp_b], 0)
    b2, a2 = up(opp_c[:, SLAB - FAR :]), down(opp_c[:, :FAR])
    opp2 = to_core(opp_c)
    ends = jnp.concatenate([b0, b1, a0, a1], 0)
    ends2 = to_core(ends)
    tail = jnp.concatenate([b2, a2], 0)
    tail2 = to_core(tail)

    def in_order(near, opp_c):
        mine, prv, nxt = near[0:2], near[2:4], near[4:6]
        return [opp_c[0:1], nxt[1:2], opp_c[1:2], prv[0:1], nxt[0:1], prv[1:2], mine]

    (smooth_own,) = lateral([in_order(near, opp_c) + in_order(near2, opp2)], x_fwd, fwd_y)
    smooth_b, smooth_a = lateral(
        [
            in_order(ends[0:6], tail[0:2]) + in_order(ends2[0:6], tail2[0:2]),
            in_order(ends[6:12], tail[2:4]) + in_order(ends2[6:12], tail2[2:4]),
        ],
        x_fwd,
        fwd_y,
    )
    smooth = (smooth_b, smooth_own, smooth_a)
    own, other = middle(smooth, (rec_before, rec_own, rec_after), tf, ta, adj_x, adj_y)
    mine = mine * jnp.exp(reduce_chunk(other, own) / 8.0)
    prev_c, next_c = lax.optimization_barrier((to_next(mine), to_prev(mine)))
    near = jnp.concatenate([mine, prev_c, next_c], 0)
    near2 = to_core(near)
    opp_c = jnp.concatenate([to_next(prev_c[0:1]), to_prev(next_c[1:2])], 0)
    opp2 = to_core(opp_c)
    return place(starts, in_order(near, opp_c) + in_order(near2, opp2))


def solution(mesh):
    return jax.shard_map(
        on_device,
        mesh=mesh,
        in_specs=(
            P("gz", None, None),
            P("view", "gz", None, None),
            P("view", None, None),
            P("view", None, None),
            P("view", None),
        ),
        out_specs=P("gz", None, None),
        check_vma=False,
    )
```

```python
import jax
import jax.numpy as jnp
from jax import lax
from jax.experimental import pallas as pl
from jax.experimental.pallas import tpu as pltpu
from jax.sharding import PartitionSpec as P

DEPTH = 33
HALF = 16
N = 128
SLAB = 48
FAR = 2 * HALF
F32 = jnp.float32
BF16 = jnp.bfloat16
MIB = 1024 * 1024
PITCH = 132
STEP = 16
QUICK = pl.CostEstimate(flops=1000, bytes_accessed=1000, transcendentals=0)
LOTS = (1, 2)


def split(x):
    hi = x.astype(BF16)
    return hi, (x - hi.astype(F32)).astype(BF16)


def left_product(operand, x):
    hi, lo = split(x)
    out = jnp.dot(operand, jnp.concatenate([hi, lo], 0), preferred_element_type=F32)
    rows = operand.shape[0] // 2
    return out[:rows] + out[rows:]


def right_product(x, operand):
    hi, lo = split(x)
    out = jnp.dot(jnp.concatenate([hi, lo], 1), operand, preferred_element_type=F32)
    cols = operand.shape[1] // 2
    return out[:, :cols] + out[:, cols:]


def two_sided(planes, left, right):
    sides = [
        left_product(left, jnp.concatenate(planes[i : i + 2], 1)) for i in range(0, len(planes), 2)
    ]
    rows = jnp.concatenate([part for s in sides for part in (s[:, :N], s[:, N:])], 0)
    return right_product(rows, right)


def region_plane(refs, z):
    blocks = []
    for ref in refs:
        if len(ref.shape) == 3:
            blocks.append(ref[z])
        else:
            blocks.extend(ref[p, z] for p in range(ref.shape[0]))
    return jnp.concatenate(blocks, 0) if len(blocks) > 1 else blocks[0]


def lateral_kernel(counts, *refs):
    total = sum(c for c, _ in counts)
    ins, lefts = refs[:total], refs[total : total + len(counts)]
    right_ref, outs = refs[total + len(counts)], refs[total + len(counts) + 1 :]
    right = right_ref[...]
    at = 0
    for (count, planes), left_ref, out in zip(counts, lefts, outs):
        region = ins[at : at + count]
        at += count
        left = left_ref[...]

        @pl.loop(0, planes // STEP)
        def _(i, region=region, out=out, left=left):
            zs = [STEP * i + j for j in range(STEP)]
            res = two_sided([region_plane(region, z) for z in zs], left, right)
            for j, z in enumerate(zs):
                out[pl.ds(z * PITCH, N), :] = res[j * N : j * N + N]


def lateral(regions, lefts, right):
    counts = []
    ins = []
    for region in regions:
        ref = region[0]
        counts.append((len(region), ref.shape[0] if ref.ndim == 3 else ref.shape[1]))
        ins.extend(region)
    return pl.pallas_call(
        lambda *refs: lateral_kernel(counts, *refs),
        out_shape=[jax.ShapeDtypeStruct((p * PITCH, N), F32) for _, p in counts],
        in_specs=[pl.BlockSpec(memory_space=pltpu.VMEM)] * (len(ins) + len(lefts) + 1),
        out_specs=[pl.BlockSpec(memory_space=pltpu.VMEM)] * len(counts),
        compiler_params=pltpu.CompilerParams(vmem_limit_bytes=8 * MIB),
        cost_estimate=QUICK,
        name="lateral",
    )(*ins, *lefts, right)


def strided(refs, a):
    return jnp.concatenate([r[pl.ds(a, r.shape[0] // PITCH, stride=PITCH), :] for r in refs], 0)


def at_row(refs, a):
    return jnp.concatenate([r[a] for r in refs], 0)


def pair(pick, refs, a):
    return jnp.concatenate([pick(refs, a), pick(refs, a + 1)], 1)


def store_back(back, a, res):
    back[pl.ds(a, SLAB, stride=PITCH), :] = res[:, :N]
    back[pl.ds(a + 1, SLAB, stride=PITCH), :] = res[:, N:]


def logs_out(back, left_ref, right_ref, owns, others):
    left = left_ref[...]
    right = right_ref[...]
    begin = 0
    for own, other in zip(owns, others):
        planes = own.shape[1]
        step = 16 if planes % 16 == 0 else 12

        @pl.loop(0, planes // step)
        def _(i, own=own, other=other, begin=begin, step=step):
            zs = [step * i + j for j in range(step)]
            sides = [back[pl.ds((begin + z) * PITCH, N), :] for z in zs]
            logs = jnp.log(two_sided(sides, left, right))
            for j, z in enumerate(zs):
                for p in range(8):
                    own[p, z] = logs[j * N + 8 * p : j * N + 8 * p + 8]
                    other[p, z] = logs[j * N + 64 + 8 * p : j * N + 64 + 8 * p + 8]

        begin += planes


def middle_kernel(sb, so, sa, mb, mo, ma, tf_ref, ta_ref, left_ref, right_ref, *outs):
    outs, back = outs[:-1], outs[-1]
    lots = len(outs) // 2
    tf = tf_ref[...]
    ta = ta_ref[...]

    @pl.loop(0, N // STEP)
    def _(i):
        firsts = [STEP * i + j for j in range(0, STEP, 2)]
        blurred = [left_product(tf, pair(strided, (sb, so, sa), a)) for a in firsts]
        ratios = []
        for a, blur in zip(firsts, blurred):
            rec = pair(at_row, (mb, mo, ma), a)
            ratios.append(jnp.where(rec > 0, rec / blur, 0.0))
        for a, ratio in zip(firsts, ratios):
            store_back(back, a, left_product(ta, ratio))

    logs_out(back, left_ref, right_ref, outs[:lots], outs[lots:])


def middle(lots, smooth, recorded, tf, ta, left, right):
    ins = (*smooth, *recorded, tf, ta, left, right)
    half = jax.ShapeDtypeStruct((8, SLAB // lots, 8, N), F32)
    res = pl.pallas_call(
        middle_kernel,
        out_shape=[half] * (2 * lots),
        in_specs=[pl.BlockSpec(memory_space=pltpu.VMEM)] * len(ins),
        out_specs=[pl.BlockSpec(memory_space=pltpu.VMEM)] * (2 * lots),
        scratch_shapes=[pltpu.VMEM((SLAB * PITCH, N), F32)],
        compiler_params=pltpu.CompilerParams(vmem_limit_bytes=12 * MIB),
        cost_estimate=QUICK,
        name="middle",
    )(*ins)
    return res[:lots], res[lots:]


def operand_rows(m):
    hi, lo = split(m)
    return jnp.concatenate([hi, lo], 0)


def twice(m, axis):
    return jnp.concatenate([m, m], axis)


def operand_cols(m):
    hi, lo = split(twice(m, 0))
    return jnp.concatenate([hi, lo], 1)


def turn(src, dst, keep=None):
    @pl.loop(0, N // 8)
    def _(i):
        at = pl.multiple_of(8 * i, 8)
        for zb in range(0, src.shape[0], 8):
            block = jnp.stack([src[z, pl.ds(at, 8), :] for z in range(zb, zb + 8)], 0)
            block = jnp.swapaxes(block, 0, 1)
            if keep is not None:
                block = jnp.where(keep > 0, block, 0.0)
            for j in range(8):
                dst[at + j, zb : zb + 8, :] = block[j]


def turn_kernel(starts, before, after, before_t, after_t):
    turn(before, before_t, starts[17])
    turn(after, after_t, starts[18])


def turned(starts, before, after):
    vmem = pl.BlockSpec(memory_space=pltpu.VMEM)
    edge = jax.ShapeDtypeStruct((N, HALF, N), F32)
    return pl.pallas_call(
        turn_kernel,
        out_shape=[edge, edge],
        in_specs=[pl.BlockSpec(memory_space=pltpu.SMEM), vmem, vmem],
        out_specs=[vmem, vmem],
        compiler_params=pltpu.CompilerParams(vmem_limit_bytes=4 * MIB),
        cost_estimate=QUICK,
        name="turn",
    )(starts, before, after)


def prep_kernel(
    starts, taps, mx_ref, my_ref, rec,
    tf, ta, x_all, x_before, x_after, x_pieces, x_before2, x_after2, adj_x, fwd_y, adj_y, rec_t, xt_ref,
):
    def toeplitz(rows, cols, flip):
        i = lax.broadcasted_iota(jnp.int32, (rows, 2 * cols), 0)
        j = lax.broadcasted_iota(jnp.int32, (rows, 2 * cols), 1)
        diag = jnp.where(j >= cols, j - cols, j) - i
        out = jnp.zeros((rows, 2 * cols), F32)
        for k in range(DEPTH):
            out = jnp.where(diag == k, taps[0, DEPTH - 1 - k if flip else k], out)
        return out

    tf[...] = operand_rows(toeplitz(SLAB + 2 * HALF, SLAB + 2 * FAR, False))
    ta[...] = operand_rows(toeplitz(SLAB, SLAB + 2 * HALF, True))
    mx = mx_ref[...]
    my = my_ref[...]
    x_all[...] = operand_rows(twice(mx, 1))
    fwd_y[...] = operand_cols(my.T)
    adj_y[...] = operand_cols(my)
    xt_ref[...] = mx.T

    def row_blocks(rows):
        return jnp.concatenate([xt_ref[pl.ds(pl.multiple_of(r, 8), 8), :] for r in rows], 0)

    pieces = row_blocks([starts[p] for p in range(16)])
    adj_x[...] = operand_rows(twice(pieces, 1))
    core = starts[16]
    halves = row_blocks([core * 64 + 8 * p for p in range(8)] + [64 - core * 64 + 8 * p for p in range(8)])
    x_pieces[...] = operand_rows(twice(pieces.T, 1))
    for rows, outs in ((halves, (x_before, x_after)), (pieces, (x_before2, x_after2))):
        for k, out in enumerate(outs):
            out[...] = operand_rows(twice(rows.T * starts[17 + k].astype(F32), 1))
    turn(rec, rec_t)


def prep(starts, taps, mx, my, rec):
    full = SLAB + 2 * HALF
    wide = SLAB + 2 * FAR
    square = jax.ShapeDtypeStruct((2 * N, 2 * N), BF16)
    outs = [
        jax.ShapeDtypeStruct((2 * full, 2 * wide), BF16),
        jax.ShapeDtypeStruct((2 * SLAB, 2 * full), BF16),
        *[square] * 9,
        jax.ShapeDtypeStruct((N, SLAB, N), F32),
    ]
    vmem = pl.BlockSpec(memory_space=pltpu.VMEM)
    smem = pl.BlockSpec(memory_space=pltpu.SMEM)
    return pl.pallas_call(
        prep_kernel,
        out_shape=outs,
        in_specs=[smem, smem, vmem, vmem, vmem],
        out_specs=[vmem] * len(outs),
        scratch_shapes=[pltpu.VMEM((N, N), F32)],
        compiler_params=pltpu.CompilerParams(vmem_limit_bytes=8 * MIB),
        cost_estimate=QUICK,
        name="prep",
    )(starts, taps, mx, my, rec)


def place_kernel(lots, starts, *refs):
    out = refs[-1]
    per = (len(refs) - 1) // lots
    for k in range(lots):
        at = 0
        for ref in refs[k * per : k * per + per]:
            planes = ref.shape[1]
            for p in range(ref.shape[0]):
                begin = pl.multiple_of(starts[at], 8)
                out[k * planes : (k + 1) * planes, pl.ds(begin, 8), :] = ref[p]
                at += 1


def place(starts, lots):
    pieces = [p for lot in lots for p in lot]
    return pl.pallas_call(
        lambda *refs: place_kernel(len(lots), *refs),
        out_shape=jax.ShapeDtypeStruct((SLAB, N, N), F32),
        in_specs=[pl.BlockSpec(memory_space=pltpu.SMEM)] + [pl.BlockSpec(memory_space=pltpu.VMEM)] * len(pieces),
        out_specs=pl.BlockSpec(memory_space=pltpu.VMEM),
        compiler_params=pltpu.CompilerParams(vmem_limit_bytes=4 * MIB),
        name="place",
    )(starts, *pieces)


def to_core(x):
    return lax.ppermute(x, "view", [(i, i ^ 1) for i in range(8)])


def to_next(x):
    return lax.ppermute(x, "view", [(i, (i + 2) % 8) for i in range(8)])


def to_prev(x):
    return lax.ppermute(x, "view", [(i, (i - 2) % 8) for i in range(8)])


def up(x):
    n = lax.axis_size("gz")
    return lax.ppermute(x, "gz", [(i, (i + 1) % n) for i in range(n)])


def down(x):
    n = lax.axis_size("gz")
    return lax.ppermute(x, "gz", [((i + 1) % n, i) for i in range(n)])


def reduce_chunk(other, own):
    total = own + to_core(other)
    from_prev = to_next(total[0:2])
    from_next = to_prev(total[2:4])
    from_prev, from_next = lax.optimization_barrier((from_prev, from_next))
    fwd_next = total[4:5] + from_prev[0:1]
    fwd_prev = total[5:6] + from_next[0:1]
    fwd_next, fwd_prev = lax.optimization_barrier((fwd_next, fwd_prev))
    last_a = to_next(fwd_next)
    last_b = to_prev(fwd_prev)
    last_a, last_b = lax.optimization_barrier((last_a, last_b))
    a = total[6:7] + from_next[1:2] + last_a
    b = total[7:8] + from_prev[1:2] + last_b
    return jnp.concatenate([a, b], 0)


def on_device(estimate, measured, lateral_x, lateral_y, depth_taps):
    view = lax.axis_index("view")
    core = lax.rem(view, 2)
    chip = lax.div(view, 2)
    recorded = measured[0]
    mx = lateral_x[0]
    my = lateral_y[0]

    nxt, prv, opp = (chip + 1) % 4, (chip + 3) % 4, (chip + 2) % 4
    order = jnp.stack([2 * opp, 2 * nxt + 1, 2 * opp + 1, 2 * prv, 2 * nxt, 2 * prv + 1, 2 * chip, 2 * chip + 1])
    slab = lax.axis_index("gz")
    more = jnp.stack([core, slab > 0, slab < lax.axis_size("gz") - 1])
    starts = jnp.concatenate([core * 64 + 8 * order, (1 - core) * 64 + 8 * order, more]).astype(jnp.int32)

    before = up(lax.dynamic_slice(estimate, (SLAB - FAR, core * 64, 0), (FAR, 64, N)))
    after = down(lax.dynamic_slice(estimate, (0, core * 64, 0), (FAR, 64, N)))
    rec_before = up(recorded[SLAB - HALF :])
    rec_after = down(recorded[:HALF])
    tf, ta, x_all, x_before, x_after, x_own, x_before2, x_after2, adj_x, fwd_y, adj_y, rec_own = prep(
        starts, depth_taps, mx, my, recorded
    )
    mine = lax.dynamic_slice(estimate, (0, core * 64 + chip * 16, 0), (SLAB, 16, N))
    mine = jnp.stack([mine[:, :8], mine[:, 8:]], 0)
    before2, after2 = to_core(before), to_core(after)

    (smooth_own,) = lateral([[estimate]], [x_all], fwd_y)
    smooth_b, smooth_a = lateral([[before, before2], [after, after2]], [x_before, x_after], fwd_y)
    rec_before, rec_after, smooth_b, smooth_a = lax.optimization_barrier((rec_before, rec_after, smooth_b, smooth_a))
    rec_before, rec_after = turned(starts, rec_before, rec_after)
    recs = (rec_before, rec_own, rec_after)

    def log_sums(update, smooth):
        owns, others = middle(LOTS[update], smooth, recs, tf, ta, adj_x, adj_y)
        return [reduce_chunk(other, own) for own, other in zip(owns, others)]

    log_sum = jnp.concatenate(log_sums(0, (smooth_b, smooth_own, smooth_a)), 1)
    mine = mine * jnp.exp(log_sum / 8.0)

    prev_c, next_c = to_next(mine), to_prev(mine)
    b0, a0 = up(mine[:, SLAB - FAR :]), down(mine[:, :FAR])
    prev_c, next_c, b0, a0 = lax.optimization_barrier((prev_c, next_c, b0, a0))
    opp_a, opp_b = to_next(prev_c[0:1]), to_prev(next_c[1:2])
    sides = jnp.concatenate([prev_c, next_c], 0)
    b1, a1 = up(sides[:, SLAB - FAR :]), down(sides[:, :FAR])
    near = jnp.concatenate([mine, sides], 0)
    near2 = to_core(near)
    opp_a, opp_b, near2 = lax.optimization_barrier((opp_a, opp_b, near2))
    opp_c = jnp.concatenate([opp_a, opp_b], 0)
    b2, a2 = up(opp_c[:, SLAB - FAR :]), down(opp_c[:, :FAR])
    opp2 = to_core(opp_c)
    ends = jnp.concatenate([b0, b1, a0, a1], 0)
    ends2 = to_core(ends)
    tail = jnp.concatenate([b2, a2], 0)
    tail2 = to_core(tail)

    def in_order(near, opp_c):
        mine, prv, nxt = near[0:2], near[2:4], near[4:6]
        return [opp_c[0:1], nxt[1:2], opp_c[1:2], prv[0:1], nxt[0:1], prv[1:2], mine]

    (smooth_own,) = lateral([in_order(near, opp_c) + in_order(near2, opp2)], [x_own], fwd_y)
    smooth_b, smooth_a = lateral(
        [
            in_order(ends[0:6], tail[0:2]) + in_order(ends2[0:6], tail2[0:2]),
            in_order(ends[6:12], tail[2:4]) + in_order(ends2[6:12], tail2[2:4]),
        ],
        [x_before2, x_after2],
        fwd_y,
    )
    lots = []
    for k, log_sum in enumerate(log_sums(1, (smooth_b, smooth_own, smooth_a))):
        planes = log_sum.shape[1]
        chunk = mine[:, k * planes : (k + 1) * planes] * jnp.exp(log_sum / 8.0)
        prev_c, next_c = lax.optimization_barrier((to_next(chunk), to_prev(chunk)))
        near = jnp.concatenate([chunk, prev_c, next_c], 0)
        near2 = to_core(near)
        opp_c = jnp.concatenate([to_next(prev_c[0:1]), to_prev(next_c[1:2])], 0)
        opp2 = to_core(opp_c)
        lots.append(in_order(near, opp_c) + in_order(near2, opp2))
    return place(starts, lots)


def solution(mesh):
    return jax.shard_map(
        on_device,
        mesh=mesh,
        in_specs=(
            P("gz", None, None),
            P("view", "gz", None, None),
            P("view", None, None),
            P("view", None, None),
            P("view", None),
        ),
        out_specs=P("gz", None, None),
        check_vma=False,
    )
```

```python
import jax
import jax.numpy as jnp
from jax import lax
from jax.experimental import pallas as pl
from jax.experimental.pallas import tpu as pltpu
from jax.sharding import PartitionSpec as P

DEPTH = 33
HALF = 16
N = 128
SLAB = 48
FAR = 2 * HALF
F32 = jnp.float32
BF16 = jnp.bfloat16
MIB = 1024 * 1024
PITCH = 132
STEP = 16
QUICK = pl.CostEstimate(flops=1000, bytes_accessed=1000, transcendentals=0)
LOTS = (1, 2)


def split(x):
    hi = x.astype(BF16)
    return hi, (x - hi.astype(F32)).astype(BF16)


def left_product(operand, x):
    hi, lo = split(x)
    out = jnp.dot(operand, jnp.concatenate([hi, lo], 0), preferred_element_type=F32)
    rows = operand.shape[0] // 2
    return out[:rows] + out[rows:]


def right_product(x, operand):
    hi, lo = split(x)
    out = jnp.dot(jnp.concatenate([hi, lo], 1), operand, preferred_element_type=F32)
    cols = operand.shape[1] // 2
    return out[:, :cols] + out[:, cols:]


def two_sided(planes, left, right):
    sides = [
        left_product(left, jnp.concatenate(planes[i : i + 2], 1)) for i in range(0, len(planes), 2)
    ]
    rows = jnp.concatenate([part for s in sides for part in (s[:, :N], s[:, N:])], 0)
    return right_product(rows, right)


def region_plane(refs, z):
    blocks = []
    for ref in refs:
        if len(ref.shape) == 3:
            blocks.append(ref[z])
        else:
            blocks.extend(ref[p, z] for p in range(ref.shape[0]))
    return jnp.concatenate(blocks, 0) if len(blocks) > 1 else blocks[0]


def lateral_kernel(counts, *refs):
    total = sum(c for c, _ in counts)
    ins, lefts = refs[:total], refs[total : total + len(counts)]
    right_ref, outs = refs[total + len(counts)], refs[total + len(counts) + 1 :]
    right = right_ref[...]
    at = 0
    for (count, planes), left_ref, out in zip(counts, lefts, outs):
        region = ins[at : at + count]
        at += count
        left = left_ref[...]

        @pl.loop(0, planes // STEP)
        def _(i, region=region, out=out, left=left):
            zs = [STEP * i + j for j in range(STEP)]
            res = two_sided([region_plane(region, z) for z in zs], left, right)
            for j, z in enumerate(zs):
                out[pl.ds(z * PITCH, N), :] = res[j * N : j * N + N]


def lateral(regions, lefts, right):
    counts = []
    ins = []
    for region in regions:
        ref = region[0]
        counts.append((len(region), ref.shape[0] if ref.ndim == 3 else ref.shape[1]))
        ins.extend(region)
    return pl.pallas_call(
        lambda *refs: lateral_kernel(counts, *refs),
        out_shape=[jax.ShapeDtypeStruct((p * PITCH, N), F32) for _, p in counts],
        in_specs=[pl.BlockSpec(memory_space=pltpu.VMEM)] * (len(ins) + len(lefts) + 1),
        out_specs=[pl.BlockSpec(memory_space=pltpu.VMEM)] * len(counts),
        compiler_params=pltpu.CompilerParams(vmem_limit_bytes=8 * MIB),
        cost_estimate=QUICK,
        name="lateral",
    )(*ins, *lefts, right)


def strided(refs, a):
    return jnp.concatenate([r[pl.ds(a, r.shape[0] // PITCH, stride=PITCH), :] for r in refs], 0)


def at_row(refs, a):
    return jnp.concatenate([r[a] for r in refs], 0)


def pair(pick, refs, a):
    return jnp.concatenate([pick(refs, a), pick(refs, a + 1)], 1)


def store_back(back, a, res):
    back[pl.ds(a, SLAB, stride=PITCH), :] = res[:, :N]
    back[pl.ds(a + 1, SLAB, stride=PITCH), :] = res[:, N:]


def logs_out(back, left_ref, right_ref, owns, others):
    left = left_ref[...]
    right = right_ref[...]
    begin = 0
    for own, other in zip(owns, others):
        planes = own.shape[1]
        step = 16 if planes % 16 == 0 else 12

        @pl.loop(0, planes // step)
        def _(i, own=own, other=other, begin=begin, step=step):
            zs = [step * i + j for j in range(step)]
            sides = [back[pl.ds((begin + z) * PITCH, N), :] for z in zs]
            logs = jnp.log(two_sided(sides, left, right))
            for j, z in enumerate(zs):
                for p in range(8):
                    own[p, z] = logs[j * N + 8 * p : j * N + 8 * p + 8]
                    other[p, z] = logs[j * N + 64 + 8 * p : j * N + 64 + 8 * p + 8]

        begin += planes


def middle_kernel(sb, so, sa, mb, mo, ma, tf_ref, ta_ref, left_ref, right_ref, *outs):
    outs, back = outs[:-1], outs[-1]
    lots = len(outs) // 2
    tf = tf_ref[...]
    ta = ta_ref[...]

    @pl.loop(0, N // STEP)
    def _(i):
        firsts = [STEP * i + j for j in range(0, STEP, 2)]
        blurred = [left_product(tf, pair(strided, (sb, so, sa), a)) for a in firsts]
        ratios = []
        for a, blur in zip(firsts, blurred):
            rec = pair(at_row, (mb, mo, ma), a)
            ratios.append(jnp.where(rec > 0, rec / blur, 0.0))
        for a, ratio in zip(firsts, ratios):
            store_back(back, a, left_product(ta, ratio))

    logs_out(back, left_ref, right_ref, outs[:lots], outs[lots:])


def middle(lots, smooth, recorded, tf, ta, left, right):
    ins = (*smooth, *recorded, tf, ta, left, right)
    half = jax.ShapeDtypeStruct((8, SLAB // lots, 8, N), F32)
    res = pl.pallas_call(
        middle_kernel,
        out_shape=[half] * (2 * lots),
        in_specs=[pl.BlockSpec(memory_space=pltpu.VMEM)] * len(ins),
        out_specs=[pl.BlockSpec(memory_space=pltpu.VMEM)] * (2 * lots),
        scratch_shapes=[pltpu.VMEM((SLAB * PITCH, N), F32)],
        compiler_params=pltpu.CompilerParams(vmem_limit_bytes=12 * MIB),
        cost_estimate=QUICK,
        name="middle",
    )(*ins)
    return res[:lots], res[lots:]


def operand_rows(m):
    hi, lo = split(m)
    return jnp.concatenate([hi, lo], 0)


def twice(m, axis):
    return jnp.concatenate([m, m], axis)


def operand_cols(m):
    hi, lo = split(twice(m, 0))
    return jnp.concatenate([hi, lo], 1)


def turn(src, dst, keep=None):
    @pl.loop(0, N // 8)
    def _(i):
        at = pl.multiple_of(8 * i, 8)
        for zb in range(0, src.shape[0], 8):
            block = jnp.stack([src[z, pl.ds(at, 8), :] for z in range(zb, zb + 8)], 0)
            block = jnp.swapaxes(block, 0, 1)
            if keep is not None:
                block = jnp.where(keep > 0, block, 0.0)
            for j in range(8):
                dst[at + j, zb : zb + 8, :] = block[j]


def turn_kernel(starts, before, after, before_t, after_t):
    turn(before, before_t, starts[49])
    turn(after, after_t, starts[50])


def turned(starts, before, after):
    vmem = pl.BlockSpec(memory_space=pltpu.VMEM)
    edge = jax.ShapeDtypeStruct((N, HALF, N), F32)
    return pl.pallas_call(
        turn_kernel,
        out_shape=[edge, edge],
        in_specs=[pl.BlockSpec(memory_space=pltpu.SMEM), vmem, vmem],
        out_specs=[vmem, vmem],
        compiler_params=pltpu.CompilerParams(vmem_limit_bytes=4 * MIB),
        cost_estimate=QUICK,
        name="turn",
    )(starts, before, after)


def prep_kernel(
    starts, taps, mx_ref, my_ref, rec,
    tf, ta, x_all, x_before, x_after, x_pieces, x_before2, x_after2, adj_x, fwd_y, adj_y, rec_t, xt_ref,
):
    def toeplitz(rows, cols, flip):
        i = lax.broadcasted_iota(jnp.int32, (rows, 2 * cols), 0)
        j = lax.broadcasted_iota(jnp.int32, (rows, 2 * cols), 1)
        diag = jnp.where(j >= cols, j - cols, j) - i
        out = jnp.zeros((rows, 2 * cols), F32)
        for k in range(DEPTH):
            out = jnp.where(diag == k, taps[0, DEPTH - 1 - k if flip else k], out)
        return out

    tf[...] = operand_rows(toeplitz(SLAB + 2 * HALF, SLAB + 2 * FAR, False))
    ta[...] = operand_rows(toeplitz(SLAB, SLAB + 2 * HALF, True))
    mx = mx_ref[...]
    my = my_ref[...]
    x_all[...] = operand_rows(twice(mx, 1))
    fwd_y[...] = operand_cols(my.T)
    adj_y[...] = operand_cols(my)
    xt_ref[...] = mx.T

    def row_blocks(rows):
        return jnp.concatenate([xt_ref[pl.ds(pl.multiple_of(r, 8), 8), :] for r in rows], 0)

    pieces = row_blocks([starts[p] for p in range(16)])
    adj_x[...] = operand_rows(twice(pieces, 1))
    x_pieces[...] = operand_rows(twice(pieces.T, 1))
    core = starts[48]
    halves = row_blocks([core * 64 + 8 * p for p in range(8)] + [64 - core * 64 + 8 * p for p in range(8)])
    for k, (out, out2) in enumerate(((x_before, x_before2), (x_after, x_after2))):
        there = starts[49 + k].astype(F32)
        out[...] = operand_rows(twice(halves.T * there, 1))
        rows = row_blocks([starts[16 + 16 * k + p] for p in range(16)])
        out2[...] = operand_rows(twice(rows.T * there, 1))
    turn(rec, rec_t)


def prep(starts, taps, mx, my, rec):
    full = SLAB + 2 * HALF
    wide = SLAB + 2 * FAR
    square = jax.ShapeDtypeStruct((2 * N, 2 * N), BF16)
    outs = [
        jax.ShapeDtypeStruct((2 * full, 2 * wide), BF16),
        jax.ShapeDtypeStruct((2 * SLAB, 2 * full), BF16),
        *[square] * 9,
        jax.ShapeDtypeStruct((N, SLAB, N), F32),
    ]
    vmem = pl.BlockSpec(memory_space=pltpu.VMEM)
    smem = pl.BlockSpec(memory_space=pltpu.SMEM)
    return pl.pallas_call(
        prep_kernel,
        out_shape=outs,
        in_specs=[smem, smem, vmem, vmem, vmem],
        out_specs=[vmem] * len(outs),
        scratch_shapes=[pltpu.VMEM((N, N), F32)],
        compiler_params=pltpu.CompilerParams(vmem_limit_bytes=8 * MIB),
        cost_estimate=QUICK,
        name="prep",
    )(starts, taps, mx, my, rec)


def place_kernel(lots, starts, *refs):
    out = refs[-1]
    per = (len(refs) - 1) // lots
    for k in range(lots):
        at = 0
        for ref in refs[k * per : k * per + per]:
            planes = ref.shape[1]
            for p in range(ref.shape[0]):
                begin = pl.multiple_of(starts[at], 8)
                out[k * planes : (k + 1) * planes, pl.ds(begin, 8), :] = ref[p]
                at += 1


def place(starts, lots):
    pieces = [p for lot in lots for p in lot]
    return pl.pallas_call(
        lambda *refs: place_kernel(len(lots), *refs),
        out_shape=jax.ShapeDtypeStruct((SLAB, N, N), F32),
        in_specs=[pl.BlockSpec(memory_space=pltpu.SMEM)] + [pl.BlockSpec(memory_space=pltpu.VMEM)] * len(pieces),
        out_specs=pl.BlockSpec(memory_space=pltpu.VMEM),
        compiler_params=pltpu.CompilerParams(vmem_limit_bytes=4 * MIB),
        name="place",
    )(starts, *pieces)


def to_core(x):
    return lax.ppermute(x, "view", [(i, i ^ 1) for i in range(8)])


def to_next(x):
    return lax.ppermute(x, "view", [(i, (i + 2) % 8) for i in range(8)])


def to_prev(x):
    return lax.ppermute(x, "view", [(i, (i - 2) % 8) for i in range(8)])


def up(x):
    n = lax.axis_size("gz")
    return lax.ppermute(x, "gz", [(i, (i + 1) % n) for i in range(n)])


def down(x):
    n = lax.axis_size("gz")
    return lax.ppermute(x, "gz", [((i + 1) % n, i) for i in range(n)])


def shift(x, step):
    n = lax.axis_size("gz")
    pairs = []
    for v in range(8):
        for g in range(n):
            turn = 0
            if v % 2 and g == (n // 2 - 1 if step > 0 else n // 2):
                turn = -2 * step
            if v % 2 and g == (n - 1 if step > 0 else 0):
                turn = 2 * step
            pairs.append((v * n + g, (v + turn) % 8 * n + (g + step) % n))
    return lax.ppermute(x, ("view", "gz"), pairs)


def reduce_chunk(other, own):
    total = own + to_core(other)
    from_prev = to_next(total[0:2])
    from_next = to_prev(total[2:4])
    from_prev, from_next = lax.optimization_barrier((from_prev, from_next))
    fwd_next = total[4:5] + from_prev[0:1]
    fwd_prev = total[5:6] + from_next[0:1]
    fwd_next, fwd_prev = lax.optimization_barrier((fwd_next, fwd_prev))
    last_a = to_next(fwd_next)
    last_b = to_prev(fwd_prev)
    last_a, last_b = lax.optimization_barrier((last_a, last_b))
    a = total[6:7] + from_next[1:2] + last_a
    b = total[7:8] + from_prev[1:2] + last_b
    return jnp.concatenate([a, b], 0)


def on_device(estimate, measured, lateral_x, lateral_y, depth_taps):
    view = lax.axis_index("view")
    core = lax.rem(view, 2)
    chip = lax.div(view, 2)
    recorded = measured[0]
    mx = lateral_x[0]
    my = lateral_y[0]

    def order(sender):
        q, nxt, prv, opp = sender % 4, (sender + 1) % 4, (sender + 3) % 4, (sender + 2) % 4
        return 8 * jnp.stack([2 * opp, 2 * nxt + 1, 2 * opp + 1, 2 * prv, 2 * nxt, 2 * prv + 1, 2 * q, 2 * q + 1])

    def halves(sender_of):
        return [core * 64 + order(sender_of(core)), (1 - core) * 64 + order(sender_of(1 - core))]

    slab = lax.axis_index("gz")
    slabs = lax.axis_size("gz")
    more = jnp.stack([core, slab > 0, slab < slabs - 1])
    starts = jnp.concatenate(
        halves(lambda c: chip)
        + halves(lambda c: chip + c * (slab == slabs // 2))
        + halves(lambda c: chip + 3 * c * (slab == slabs // 2 - 1))
        + [more]
    ).astype(jnp.int32)

    before = shift(lax.dynamic_slice(estimate, (SLAB - FAR, core * 64, 0), (FAR, 64, N)), 1)
    after = shift(lax.dynamic_slice(estimate, (0, core * 64, 0), (FAR, 64, N)), -1)
    rec_before = up(recorded[SLAB - HALF :])
    rec_after = down(recorded[:HALF])
    tf, ta, x_all, x_before, x_after, x_own, x_before2, x_after2, adj_x, fwd_y, adj_y, rec_own = prep(
        starts, depth_taps, mx, my, recorded
    )
    mine = lax.dynamic_slice(estimate, (0, core * 64 + chip * 16, 0), (SLAB, 16, N))
    mine = jnp.stack([mine[:, :8], mine[:, 8:]], 0)
    before2, after2 = to_core(before), to_core(after)

    (smooth_own,) = lateral([[estimate]], [x_all], fwd_y)
    smooth_b, smooth_a = lateral([[before, before2], [after, after2]], [x_before, x_after], fwd_y)
    rec_before, rec_after, smooth_b, smooth_a, mine = lax.optimization_barrier(
        (rec_before, rec_after, smooth_b, smooth_a, mine)
    )
    rec_before, rec_after = turned(starts, rec_before, rec_after)
    recs = (rec_before, rec_own, rec_after)

    def log_sums(update, smooth):
        owns, others = middle(LOTS[update], smooth, recs, tf, ta, adj_x, adj_y)
        return [reduce_chunk(other, own) for own, other in zip(owns, others)]

    log_sum = jnp.concatenate(log_sums(0, (smooth_b, smooth_own, smooth_a)), 1)
    mine = mine * jnp.exp(log_sum / 8.0)

    prev_c, next_c = lax.optimization_barrier((to_next(mine), to_prev(mine)))
    opp_a, opp_b = to_next(prev_c[0:1]), to_prev(next_c[1:2])
    near = jnp.concatenate([mine, prev_c, next_c], 0)
    b1, a1 = shift(near[:, SLAB - FAR :], 1), shift(near[:, :FAR], -1)
    near2 = to_core(near)
    opp_a, opp_b, near2 = lax.optimization_barrier((opp_a, opp_b, near2))
    opp_c = jnp.concatenate([opp_a, opp_b], 0)
    b2, a2 = shift(opp_c[:, SLAB - FAR :], 1), shift(opp_c[:, :FAR], -1)
    opp2 = to_core(opp_c)
    ends = jnp.concatenate([b1, a1], 0)
    ends2 = to_core(ends)
    tail = jnp.concatenate([b2, a2], 0)
    tail2 = to_core(tail)

    def in_order(near, opp_c):
        mine, prv, nxt = near[0:2], near[2:4], near[4:6]
        return [opp_c[0:1], nxt[1:2], opp_c[1:2], prv[0:1], nxt[0:1], prv[1:2], mine]

    (smooth_own,) = lateral([in_order(near, opp_c) + in_order(near2, opp2)], [x_own], fwd_y)
    smooth_b, smooth_a = lateral(
        [
            in_order(ends[0:6], tail[0:2]) + in_order(ends2[0:6], tail2[0:2]),
            in_order(ends[6:12], tail[2:4]) + in_order(ends2[6:12], tail2[2:4]),
        ],
        [x_before2, x_after2],
        fwd_y,
    )
    lots = []
    for k, log_sum in enumerate(log_sums(1, (smooth_b, smooth_own, smooth_a))):
        planes = log_sum.shape[1]
        chunk = mine[:, k * planes : (k + 1) * planes] * jnp.exp(log_sum / 8.0)
        prev_c, next_c = lax.optimization_barrier((to_next(chunk), to_prev(chunk)))
        near = jnp.concatenate([chunk, prev_c, next_c], 0)
        near2 = to_core(near)
        opp_c = jnp.concatenate([to_next(prev_c[0:1]), to_prev(next_c[1:2])], 0)
        opp2 = to_core(opp_c)
        lots.append(in_order(near, opp_c) + in_order(near2, opp2))
    return place(starts, lots)


def solution(mesh):
    return jax.shard_map(
        on_device,
        mesh=mesh,
        in_specs=(
            P("gz", None, None),
            P("view", "gz", None, None),
            P("view", None, None),
            P("view", None, None),
            P("view", None),
        ),
        out_specs=P("gz", None, None),
        check_vma=False,
    )
```

```python
import jax
import jax.numpy as jnp
from jax import lax
from jax.experimental import pallas as pl
from jax.experimental.pallas import tpu as pltpu
from jax.sharding import PartitionSpec as P

DEPTH = 33
HALF = 16
N = 128
SLAB = 48
FAR = 2 * HALF
F32 = jnp.float32
BF16 = jnp.bfloat16
MIB = 1024 * 1024
PITCH = 132
STEP = 16
QUICK = pl.CostEstimate(flops=1000, bytes_accessed=1000, transcendentals=0)
LOTS = (1, 1)


def split(x):
    hi = x.astype(BF16)
    return hi, (x - hi.astype(F32)).astype(BF16)


def left_product(operand, x):
    hi, lo = split(x)
    out = jnp.dot(operand, jnp.concatenate([hi, lo], 0), preferred_element_type=F32)
    rows = operand.shape[0] // 2
    return out[:rows] + out[rows:]


def right_product(x, operand):
    hi, lo = split(x)
    out = jnp.dot(jnp.concatenate([hi, lo], 1), operand, preferred_element_type=F32)
    cols = operand.shape[1] // 2
    return out[:, :cols] + out[:, cols:]


def two_sided(planes, left, right):
    sides = [
        left_product(left, jnp.concatenate(planes[i : i + 2], 1)) for i in range(0, len(planes), 2)
    ]
    rows = jnp.concatenate([part for s in sides for part in (s[:, :N], s[:, N:])], 0)
    return right_product(rows, right)


def region_plane(refs, z):
    blocks = []
    for ref in refs:
        if len(ref.shape) == 3:
            blocks.append(ref[z])
        else:
            blocks.extend(ref[p, z] for p in range(ref.shape[0]))
    return jnp.concatenate(blocks, 0) if len(blocks) > 1 else blocks[0]


def lateral_kernel(counts, *refs):
    total = sum(c for c, _ in counts)
    ins, lefts = refs[:total], refs[total : total + len(counts)]
    right_ref, outs = refs[total + len(counts)], refs[total + len(counts) + 1 :]
    right = right_ref[...]
    at = 0
    for (count, planes), left_ref, out in zip(counts, lefts, outs):
        region = ins[at : at + count]
        at += count
        left = left_ref[...]

        @pl.loop(0, planes // STEP)
        def _(i, region=region, out=out, left=left):
            zs = [STEP * i + j for j in range(STEP)]
            res = two_sided([region_plane(region, z) for z in zs], left, right)
            for j, z in enumerate(zs):
                out[pl.ds(z * PITCH, N), :] = res[j * N : j * N + N]


def lateral(regions, lefts, right):
    counts = []
    ins = []
    for region in regions:
        ref = region[0]
        counts.append((len(region), ref.shape[0] if ref.ndim == 3 else ref.shape[1]))
        ins.extend(region)
    return pl.pallas_call(
        lambda *refs: lateral_kernel(counts, *refs),
        out_shape=[jax.ShapeDtypeStruct((p * PITCH, N), F32) for _, p in counts],
        in_specs=[pl.BlockSpec(memory_space=pltpu.VMEM)] * (len(ins) + len(lefts) + 1),
        out_specs=[pl.BlockSpec(memory_space=pltpu.VMEM)] * len(counts),
        compiler_params=pltpu.CompilerParams(vmem_limit_bytes=8 * MIB),
        cost_estimate=QUICK,
        name="lateral",
    )(*ins, *lefts, right)


def strided(refs, a):
    return jnp.concatenate([r[pl.ds(a, r.shape[0] // PITCH, stride=PITCH), :] for r in refs], 0)


def at_row(refs, a):
    return jnp.concatenate([r[a] for r in refs], 0)


def pair(pick, refs, a):
    return jnp.concatenate([pick(refs, a), pick(refs, a + 1)], 1)


def store_back(back, a, res):
    back[pl.ds(a, SLAB, stride=PITCH), :] = res[:, :N]
    back[pl.ds(a + 1, SLAB, stride=PITCH), :] = res[:, N:]


def logs_out(back, left_ref, right_ref, owns, others):
    left = left_ref[...]
    right = right_ref[...]
    begin = 0
    for own, other in zip(owns, others):
        planes = own.shape[1]
        step = 16 if planes % 16 == 0 else 12

        @pl.loop(0, planes // step)
        def _(i, own=own, other=other, begin=begin, step=step):
            zs = [step * i + j for j in range(step)]
            sides = [back[pl.ds((begin + z) * PITCH, N), :] for z in zs]
            logs = jnp.log(two_sided(sides, left, right))
            for j, z in enumerate(zs):
                for p in range(8):
                    own[p, z] = logs[j * N + 8 * p : j * N + 8 * p + 8]
                    other[p, z] = logs[j * N + 64 + 8 * p : j * N + 64 + 8 * p + 8]

        begin += planes


def middle_kernel(sb, so, sa, mb, mo, ma, tf_ref, ta_ref, left_ref, right_ref, *outs):
    outs, back = outs[:-1], outs[-1]
    lots = len(outs) // 2
    tf = tf_ref[...]
    ta = ta_ref[...]

    @pl.loop(0, N // STEP)
    def _(i):
        firsts = [STEP * i + j for j in range(0, STEP, 2)]
        blurred = [left_product(tf, pair(strided, (sb, so, sa), a)) for a in firsts]
        ratios = []
        for a, blur in zip(firsts, blurred):
            rec = pair(at_row, (mb, mo, ma), a)
            ratios.append(jnp.where(rec > 0, rec / blur, 0.0))
        for a, ratio in zip(firsts, ratios):
            store_back(back, a, left_product(ta, ratio))

    logs_out(back, left_ref, right_ref, outs[:lots], outs[lots:])


def middle(lots, smooth, recorded, tf, ta, left, right):
    ins = (*smooth, *recorded, tf, ta, left, right)
    half = jax.ShapeDtypeStruct((8, SLAB // lots, 8, N), F32)
    res = pl.pallas_call(
        middle_kernel,
        out_shape=[half] * (2 * lots),
        in_specs=[pl.BlockSpec(memory_space=pltpu.VMEM)] * len(ins),
        out_specs=[pl.BlockSpec(memory_space=pltpu.VMEM)] * (2 * lots),
        scratch_shapes=[pltpu.VMEM((SLAB * PITCH, N), F32)],
        compiler_params=pltpu.CompilerParams(vmem_limit_bytes=12 * MIB),
        cost_estimate=QUICK,
        name="middle",
    )(*ins)
    return res[:lots], res[lots:]


def operand_rows(m):
    hi, lo = split(m)
    return jnp.concatenate([hi, lo], 0)


def twice(m, axis):
    return jnp.concatenate([m, m], axis)


def operand_cols(m):
    hi, lo = split(twice(m, 0))
    return jnp.concatenate([hi, lo], 1)


def turn(src, dst, keep=None):
    @pl.loop(0, N // 8)
    def _(i):
        at = pl.multiple_of(8 * i, 8)
        for zb in range(0, src.shape[0], 8):
            block = jnp.stack([src[z, pl.ds(at, 8), :] for z in range(zb, zb + 8)], 0)
            block = jnp.swapaxes(block, 0, 1)
            if keep is not None:
                block = jnp.where(keep > 0, block, 0.0)
            for j in range(8):
                dst[at + j, zb : zb + 8, :] = block[j]


def turn_kernel(starts, before, after, before_t, after_t):
    turn(before, before_t, starts[49])
    turn(after, after_t, starts[50])


def turned(starts, before, after):
    vmem = pl.BlockSpec(memory_space=pltpu.VMEM)
    edge = jax.ShapeDtypeStruct((N, HALF, N), F32)
    return pl.pallas_call(
        turn_kernel,
        out_shape=[edge, edge],
        in_specs=[pl.BlockSpec(memory_space=pltpu.SMEM), vmem, vmem],
        out_specs=[vmem, vmem],
        compiler_params=pltpu.CompilerParams(vmem_limit_bytes=4 * MIB),
        cost_estimate=QUICK,
        name="turn",
    )(starts, before, after)


def prep_kernel(
    starts, taps, mx_ref, my_ref, rec,
    tf, ta, x_all, x_before, x_after, x_pieces, x_before2, x_after2, adj_x, fwd_y, adj_y, rec_t, xt_ref,
):
    def toeplitz(rows, cols, flip):
        i = lax.broadcasted_iota(jnp.int32, (rows, 2 * cols), 0)
        j = lax.broadcasted_iota(jnp.int32, (rows, 2 * cols), 1)
        diag = jnp.where(j >= cols, j - cols, j) - i
        out = jnp.zeros((rows, 2 * cols), F32)
        for k in range(DEPTH):
            out = jnp.where(diag == k, taps[0, DEPTH - 1 - k if flip else k], out)
        return out

    tf[...] = operand_rows(toeplitz(SLAB + 2 * HALF, SLAB + 2 * FAR, False))
    ta[...] = operand_rows(toeplitz(SLAB, SLAB + 2 * HALF, True))
    mx = mx_ref[...]
    my = my_ref[...]
    x_all[...] = operand_rows(twice(mx, 1))
    fwd_y[...] = operand_cols(my.T)
    adj_y[...] = operand_cols(my)
    xt_ref[...] = mx.T

    def row_blocks(rows):
        return jnp.concatenate([xt_ref[pl.ds(pl.multiple_of(r, 8), 8), :] for r in rows], 0)

    pieces = row_blocks([starts[p] for p in range(16)])
    adj_x[...] = operand_rows(twice(pieces, 1))
    x_pieces[...] = operand_rows(twice(pieces.T, 1))
    core = starts[48]
    halves = row_blocks([core * 64 + 8 * p for p in range(8)] + [64 - core * 64 + 8 * p for p in range(8)])
    for k, (out, out2) in enumerate(((x_before, x_before2), (x_after, x_after2))):
        there = starts[49 + k].astype(F32)
        out[...] = operand_rows(twice(halves.T * there, 1))
        rows = row_blocks([starts[16 + 16 * k + p] for p in range(16)])
        out2[...] = operand_rows(twice(rows.T * there, 1))
    turn(rec, rec_t)


def prep(starts, taps, mx, my, rec):
    full = SLAB + 2 * HALF
    wide = SLAB + 2 * FAR
    square = jax.ShapeDtypeStruct((2 * N, 2 * N), BF16)
    outs = [
        jax.ShapeDtypeStruct((2 * full, 2 * wide), BF16),
        jax.ShapeDtypeStruct((2 * SLAB, 2 * full), BF16),
        *[square] * 9,
        jax.ShapeDtypeStruct((N, SLAB, N), F32),
    ]
    vmem = pl.BlockSpec(memory_space=pltpu.VMEM)
    smem = pl.BlockSpec(memory_space=pltpu.SMEM)
    return pl.pallas_call(
        prep_kernel,
        out_shape=outs,
        in_specs=[smem, smem, vmem, vmem, vmem],
        out_specs=[vmem] * len(outs),
        scratch_shapes=[pltpu.VMEM((N, N), F32)],
        compiler_params=pltpu.CompilerParams(vmem_limit_bytes=8 * MIB),
        cost_estimate=QUICK,
        name="prep",
    )(starts, taps, mx, my, rec)


def place_kernel(lots, starts, *refs):
    out = refs[-1]
    per = (len(refs) - 1) // lots
    for k in range(lots):
        at = 0
        for ref in refs[k * per : k * per + per]:
            planes = ref.shape[1]
            for p in range(ref.shape[0]):
                begin = pl.multiple_of(starts[at], 8)
                out[k * planes : (k + 1) * planes, pl.ds(begin, 8), :] = ref[p]
                at += 1


def place(starts, lots):
    pieces = [p for lot in lots for p in lot]
    return pl.pallas_call(
        lambda *refs: place_kernel(len(lots), *refs),
        out_shape=jax.ShapeDtypeStruct((SLAB, N, N), F32),
        in_specs=[pl.BlockSpec(memory_space=pltpu.SMEM)] + [pl.BlockSpec(memory_space=pltpu.VMEM)] * len(pieces),
        out_specs=pl.BlockSpec(memory_space=pltpu.VMEM),
        compiler_params=pltpu.CompilerParams(vmem_limit_bytes=4 * MIB),
        name="place",
    )(starts, *pieces)


def to_core(x):
    return lax.ppermute(x, "view", [(i, i ^ 1) for i in range(8)])


def to_next(x):
    return lax.ppermute(x, "view", [(i, (i + 2) % 8) for i in range(8)])


def to_prev(x):
    return lax.ppermute(x, "view", [(i, (i - 2) % 8) for i in range(8)])


def up(x):
    n = lax.axis_size("gz")
    return lax.ppermute(x, "gz", [(i, (i + 1) % n) for i in range(n)])


def down(x):
    n = lax.axis_size("gz")
    return lax.ppermute(x, "gz", [((i + 1) % n, i) for i in range(n)])


def shift(x, step):
    n = lax.axis_size("gz")
    pairs = []
    for v in range(8):
        for g in range(n):
            turn = 0
            if v % 2 and g == (n // 2 - 1 if step > 0 else n // 2):
                turn = -2 * step
            if v % 2 and g == (n - 1 if step > 0 else 0):
                turn = 2 * step
            pairs.append((v * n + g, (v + turn) % 8 * n + (g + step) % n))
    return lax.ppermute(x, ("view", "gz"), pairs)


def reduce_chunk(other, own):
    total = own + to_core(other)
    from_prev = to_next(total[0:2])
    from_next = to_prev(total[2:4])
    from_prev, from_next = lax.optimization_barrier((from_prev, from_next))
    fwd_next = total[4:5] + from_prev[0:1]
    fwd_prev = total[5:6] + from_next[0:1]
    fwd_next, fwd_prev = lax.optimization_barrier((fwd_next, fwd_prev))
    last_a = to_next(fwd_next)
    last_b = to_prev(fwd_prev)
    last_a, last_b = lax.optimization_barrier((last_a, last_b))
    a = total[6:7] + from_next[1:2] + last_a
    b = total[7:8] + from_prev[1:2] + last_b
    return jnp.concatenate([a, b], 0)


def on_device(estimate, measured, lateral_x, lateral_y, depth_taps):
    view = lax.axis_index("view")
    core = lax.rem(view, 2)
    chip = lax.div(view, 2)
    recorded = measured[0]
    mx = lateral_x[0]
    my = lateral_y[0]

    def order(sender):
        q, nxt, prv, opp = sender % 4, (sender + 1) % 4, (sender + 3) % 4, (sender + 2) % 4
        return 8 * jnp.stack([2 * opp, 2 * nxt + 1, 2 * opp + 1, 2 * prv, 2 * nxt, 2 * prv + 1, 2 * q, 2 * q + 1])

    def halves(sender_of):
        return [core * 64 + order(sender_of(core)), (1 - core) * 64 + order(sender_of(1 - core))]

    slab = lax.axis_index("gz")
    slabs = lax.axis_size("gz")
    more = jnp.stack([core, slab > 0, slab < slabs - 1])
    starts = jnp.concatenate(
        halves(lambda c: chip)
        + halves(lambda c: chip + c * (slab == slabs // 2))
        + halves(lambda c: chip + 3 * c * (slab == slabs // 2 - 1))
        + [more]
    ).astype(jnp.int32)

    before = shift(lax.dynamic_slice(estimate, (SLAB - FAR, core * 64, 0), (FAR, 64, N)), 1)
    after = shift(lax.dynamic_slice(estimate, (0, core * 64, 0), (FAR, 64, N)), -1)
    rec_before = up(recorded[SLAB - HALF :])
    rec_after = down(recorded[:HALF])
    tf, ta, x_all, x_before, x_after, x_own, x_before2, x_after2, adj_x, fwd_y, adj_y, rec_own = prep(
        starts, depth_taps, mx, my, recorded
    )
    mine = lax.dynamic_slice(estimate, (0, core * 64 + chip * 16, 0), (SLAB, 16, N))
    mine = jnp.stack([mine[:, :8], mine[:, 8:]], 0)
    before2, after2 = to_core(before), to_core(after)

    (smooth_own,) = lateral([[estimate]], [x_all], fwd_y)
    smooth_b, smooth_a = lateral([[before, before2], [after, after2]], [x_before, x_after], fwd_y)
    rec_before, rec_after, smooth_b, smooth_a, mine = lax.optimization_barrier(
        (rec_before, rec_after, smooth_b, smooth_a, mine)
    )
    rec_before, rec_after = turned(starts, rec_before, rec_after)
    recs = (rec_before, rec_own, rec_after)

    def log_sums(update, smooth):
        owns, others = middle(LOTS[update], smooth, recs, tf, ta, adj_x, adj_y)
        return [reduce_chunk(other, own) for own, other in zip(owns, others)]

    log_sum = jnp.concatenate(log_sums(0, (smooth_b, smooth_own, smooth_a)), 1)
    mine = mine * jnp.exp(log_sum / 8.0)

    prev_c, next_c = lax.optimization_barrier((to_next(mine), to_prev(mine)))
    opp_a, opp_b = to_next(prev_c[0:1]), to_prev(next_c[1:2])
    near = jnp.concatenate([mine, prev_c, next_c], 0)
    b1, a1 = shift(near[:, SLAB - FAR :], 1), shift(near[:, :FAR], -1)
    near2 = to_core(near)
    opp_a, opp_b, near2 = lax.optimization_barrier((opp_a, opp_b, near2))
    opp_c = jnp.concatenate([opp_a, opp_b], 0)
    b2, a2 = shift(opp_c[:, SLAB - FAR :], 1), shift(opp_c[:, :FAR], -1)
    opp2 = to_core(opp_c)
    ends = jnp.concatenate([b1, a1], 0)
    ends2 = to_core(ends)
    tail = jnp.concatenate([b2, a2], 0)
    tail2 = to_core(tail)

    def in_order(near, opp_c):
        mine, prv, nxt = near[0:2], near[2:4], near[4:6]
        return [opp_c[0:1], nxt[1:2], opp_c[1:2], prv[0:1], nxt[0:1], prv[1:2], mine]

    (smooth_own,) = lateral([in_order(near, opp_c) + in_order(near2, opp2)], [x_own], fwd_y)
    smooth_b, smooth_a = lateral(
        [
            in_order(ends[0:6], tail[0:2]) + in_order(ends2[0:6], tail2[0:2]),
            in_order(ends[6:12], tail[2:4]) + in_order(ends2[6:12], tail2[2:4]),
        ],
        [x_before2, x_after2],
        fwd_y,
    )
    lots = []
    for k, log_sum in enumerate(log_sums(1, (smooth_b, smooth_own, smooth_a))):
        planes = log_sum.shape[1]
        chunk = mine[:, k * planes : (k + 1) * planes] * jnp.exp(log_sum / 8.0)
        prev_c, next_c = lax.optimization_barrier((to_next(chunk), to_prev(chunk)))
        near = jnp.concatenate([chunk, prev_c, next_c], 0)
        near2 = to_core(near)
        opp_c = jnp.concatenate([to_next(prev_c[0:1]), to_prev(next_c[1:2])], 0)
        opp2 = to_core(opp_c)
        lots.append(in_order(near, opp_c) + in_order(near2, opp2))
    return place(starts, lots)


def solution(mesh):
    return jax.shard_map(
        on_device,
        mesh=mesh,
        in_specs=(
            P("gz", None, None),
            P("view", "gz", None, None),
            P("view", None, None),
            P("view", None, None),
            P("view", None),
        ),
        out_specs=P("gz", None, None),
        check_vma=False,
    )
```

```python
import jax
import jax.numpy as jnp
from jax import lax
from jax.experimental import pallas as pl
from jax.experimental.pallas import tpu as pltpu
from jax.sharding import PartitionSpec as P

DEPTH = 33
HALF = 16
N = 128
SLAB = 48
FAR = 2 * HALF
F32 = jnp.float32
BF16 = jnp.bfloat16
MIB = 1024 * 1024
PITCH = 132
STEP = 16
LOTS = (1, 2)


def split(x):
    hi = x.astype(BF16)
    return hi, (x - hi.astype(F32)).astype(BF16)


def left_product(operand, x):
    hi, lo = split(x)
    out = jnp.dot(operand, jnp.concatenate([hi, lo], 0), preferred_element_type=F32)
    rows = operand.shape[0] // 2
    return out[:rows] + out[rows:]


def right_product(x, operand):
    hi, lo = split(x)
    out = jnp.dot(jnp.concatenate([hi, lo], 1), operand, preferred_element_type=F32)
    cols = operand.shape[1] // 2
    return out[:, :cols] + out[:, cols:]


def two_sided(planes, left, right):
    sides = [
        left_product(left, jnp.concatenate(planes[i : i + 2], 1)) for i in range(0, len(planes), 2)
    ]
    rows = jnp.concatenate([part for s in sides for part in (s[:, :N], s[:, N:])], 0)
    return right_product(rows, right)


def region_plane(refs, z):
    blocks = []
    for ref in refs:
        if len(ref.shape) == 3:
            blocks.append(ref[z])
        else:
            blocks.extend(ref[p, z] for p in range(ref.shape[0]))
    return jnp.concatenate(blocks, 0) if len(blocks) > 1 else blocks[0]


def lateral_kernel(counts, *refs):
    total = sum(c for c, _ in counts)
    ins, (left_ref, right_ref), outs = refs[:total], refs[total : total + 2], refs[total + 2 :]
    left = left_ref[...]
    right = right_ref[...]
    at = 0
    for (count, planes), out in zip(counts, outs):
        region = ins[at : at + count]
        at += count

        @pl.loop(0, planes // STEP)
        def _(i, region=region, out=out):
            zs = [STEP * i + j for j in range(STEP)]
            res = two_sided([region_plane(region, z) for z in zs], left, right)
            for j, z in enumerate(zs):
                out[pl.ds(z * PITCH, N), :] = res[j * N : j * N + N]


def lateral(regions, left, right):
    counts = []
    ins = []
    for region in regions:
        ref = region[0]
        counts.append((len(region), ref.shape[0] if ref.ndim == 3 else ref.shape[1]))
        ins.extend(region)
    planes = sum(p for _, p in counts)
    return pl.pallas_call(
        lambda *refs: lateral_kernel(counts, *refs),
        out_shape=[jax.ShapeDtypeStruct((p * PITCH, N), F32) for _, p in counts],
        in_specs=[pl.BlockSpec(memory_space=pltpu.VMEM)] * (len(ins) + 2),
        out_specs=[pl.BlockSpec(memory_space=pltpu.VMEM)] * len(counts),
        compiler_params=pltpu.CompilerParams(vmem_limit_bytes=24 * MIB),
        cost_estimate=pl.CostEstimate(flops=planes * 16 * N**3, bytes_accessed=planes * 8 * N * N, transcendentals=0),
        name="lateral",
    )(*ins, left, right)


def strided(refs, a):
    return jnp.concatenate([r[pl.ds(a, r.shape[0] // PITCH, stride=PITCH), :] for r in refs], 0)


def at_row(refs, a):
    return jnp.concatenate([r[a] for r in refs], 0)


def pair(pick, refs, a):
    return jnp.concatenate([pick(refs, a), pick(refs, a + 1)], 1)


def store_back(back, a, res):
    back[pl.ds(a, SLAB, stride=PITCH), :] = res[:, :N]
    back[pl.ds(a + 1, SLAB, stride=PITCH), :] = res[:, N:]


def logs_out(back, left_ref, right_ref, owns, others):
    left = left_ref[...]
    right = right_ref[...]
    begin = 0
    for own, other in zip(owns, others):
        planes = own.shape[1]
        step = 16 if planes % 16 == 0 else 8

        @pl.loop(0, planes // step)
        def _(i, own=own, other=other, begin=begin, step=step):
            zs = [step * i + j for j in range(step)]
            sides = [back[pl.ds((begin + z) * PITCH, N), :] for z in zs]
            logs = jnp.log(two_sided(sides, left, right))
            for j, z in enumerate(zs):
                for p in range(8):
                    own[p, z] = logs[j * N + 8 * p : j * N + 8 * p + 8]
                    other[p, z] = logs[j * N + 64 + 8 * p : j * N + 64 + 8 * p + 8]

        begin += planes


def middle_kernel(sb, so, sa, mb, mo, ma, tf_ref, ta_ref, left_ref, right_ref, *outs):
    outs, back = outs[:-1], outs[-1]
    lots = len(outs) // 2
    tf = tf_ref[...]
    ta = ta_ref[...]

    @pl.loop(0, N // STEP)
    def _(i):
        firsts = [STEP * i + j for j in range(0, STEP, 2)]
        blurred = [left_product(tf, pair(strided, (sb, so, sa), a)) for a in firsts]
        ratios = []
        for a, blur in zip(firsts, blurred):
            rec = pair(at_row, (mb, mo, ma), a)
            ratios.append(jnp.where(rec > 0, rec / blur, 0.0))
        for a, ratio in zip(firsts, ratios):
            store_back(back, a, left_product(ta, ratio))

    logs_out(back, left_ref, right_ref, outs[:lots], outs[lots:])


def middle(lots, smooth, recorded, tf, ta, left, right):
    ins = (*smooth, *recorded, tf, ta, left, right)
    half = jax.ShapeDtypeStruct((8, SLAB // lots, 8, N), F32)
    res = pl.pallas_call(
        middle_kernel,
        out_shape=[half] * (2 * lots),
        in_specs=[pl.BlockSpec(memory_space=pltpu.VMEM)] * len(ins),
        out_specs=[pl.BlockSpec(memory_space=pltpu.VMEM)] * (2 * lots),
        scratch_shapes=[pltpu.VMEM((SLAB * PITCH, N), F32)],
        compiler_params=pltpu.CompilerParams(vmem_limit_bytes=32 * MIB),
        cost_estimate=pl.CostEstimate(flops=8 * 10**9, bytes_accessed=15 * MIB, transcendentals=SLAB * N * N),
        name="middle",
    )(*ins)
    return res[:lots], res[lots:]


def operand_rows(m):
    hi, lo = split(m)
    return jnp.concatenate([hi, lo], 0)


def twice(m, axis):
    return jnp.concatenate([m, m], axis)


def operand_cols(m):
    hi, lo = split(twice(m, 0))
    return jnp.concatenate([hi, lo], 1)


def prep_kernel(
    starts, taps, mx_ref, my_ref, rec,
    tf, ta, x_all, x_halves, x_pieces, adj_x, fwd_y, adj_y, rec_t, rec_first, rec_last, xt_ref,
):
    def toeplitz(rows, cols, flip):
        i = lax.broadcasted_iota(jnp.int32, (rows, 2 * cols), 0)
        j = lax.broadcasted_iota(jnp.int32, (rows, 2 * cols), 1)
        diag = jnp.where(j >= cols, j - cols, j) - i
        out = jnp.zeros((rows, 2 * cols), F32)
        for k in range(DEPTH):
            out = jnp.where(diag == k, taps[0, DEPTH - 1 - k if flip else k], out)
        return out

    tf[...] = operand_rows(toeplitz(SLAB + 2 * HALF, SLAB + 2 * FAR, False))
    ta[...] = operand_rows(toeplitz(SLAB, SLAB + 2 * HALF, True))
    mx = mx_ref[...]
    my = my_ref[...]
    x_all[...] = operand_rows(twice(mx, 1))
    fwd_y[...] = operand_cols(my.T)
    adj_y[...] = operand_cols(my)
    xt_ref[...] = mx.T

    def row_blocks(rows):
        return jnp.concatenate([xt_ref[pl.ds(pl.multiple_of(r, 8), 8), :] for r in rows], 0)

    pieces = row_blocks([starts[p] for p in range(16)])
    adj_x[...] = operand_rows(twice(pieces, 1))
    x_pieces[...] = operand_rows(twice(pieces.T, 1))
    core = starts[16]
    halves = row_blocks([core * 64 + 8 * p for p in range(8)] + [64 - core * 64 + 8 * p for p in range(8)])
    x_halves[...] = operand_rows(twice(halves.T, 1))

    @pl.loop(0, N // 8)
    def _(i):
        at = pl.multiple_of(8 * i, 8)
        for zb in range(0, SLAB, 8):
            block = jnp.stack([rec[z, pl.ds(at, 8), :] for z in range(zb, zb + 8)], 0)
            block = jnp.swapaxes(block, 0, 1)
            for j in range(8):
                rec_t[at + j, zb : zb + 8, :] = block[j]
                if zb < HALF:
                    rec_first[at + j, zb : zb + 8, :] = block[j]
                if zb >= SLAB - HALF:
                    rec_last[at + j, zb - SLAB + HALF : zb - SLAB + HALF + 8, :] = block[j]


def prep(starts, taps, mx, my, rec):
    full = SLAB + 2 * HALF
    wide = SLAB + 2 * FAR
    square = jax.ShapeDtypeStruct((2 * N, 2 * N), BF16)
    edge = jax.ShapeDtypeStruct((N, HALF, N), F32)
    outs = [
        jax.ShapeDtypeStruct((2 * full, 2 * wide), BF16),
        jax.ShapeDtypeStruct((2 * SLAB, 2 * full), BF16),
        *[square] * 6,
        jax.ShapeDtypeStruct((N, SLAB, N), F32),
        edge,
        edge,
    ]
    vmem = pl.BlockSpec(memory_space=pltpu.VMEM)
    smem = pl.BlockSpec(memory_space=pltpu.SMEM)
    return pl.pallas_call(
        prep_kernel,
        out_shape=outs,
        in_specs=[smem, smem, vmem, vmem, vmem],
        out_specs=[vmem] * len(outs),
        scratch_shapes=[pltpu.VMEM((N, N), F32)],
        compiler_params=pltpu.CompilerParams(vmem_limit_bytes=20 * MIB),
        name="prep",
    )(starts, taps, mx, my, rec)


def place_kernel(lots, starts, *refs):
    out = refs[-1]
    per = (len(refs) - 1) // lots
    for k in range(lots):
        at = 0
        for ref in refs[k * per : k * per + per]:
            planes = ref.shape[1]
            for p in range(ref.shape[0]):
                begin = pl.multiple_of(starts[at], 8)
                out[k * planes : (k + 1) * planes, pl.ds(begin, 8), :] = ref[p]
                at += 1


def place(starts, lots):
    pieces = [p for lot in lots for p in lot]
    return pl.pallas_call(
        lambda *refs: place_kernel(len(lots), *refs),
        out_shape=jax.ShapeDtypeStruct((SLAB, N, N), F32),
        in_specs=[pl.BlockSpec(memory_space=pltpu.SMEM)] + [pl.BlockSpec(memory_space=pltpu.VMEM)] * len(pieces),
        out_specs=pl.BlockSpec(memory_space=pltpu.VMEM),
        compiler_params=pltpu.CompilerParams(vmem_limit_bytes=4 * MIB),
        name="place",
    )(starts, *pieces)


def to_core(x):
    return lax.ppermute(x, "view", [(i, i ^ 1) for i in range(8)])


def to_next(x):
    return lax.ppermute(x, "view", [(i, (i + 2) % 8) for i in range(8)])


def to_prev(x):
    return lax.ppermute(x, "view", [(i, (i - 2) % 8) for i in range(8)])


def up(x):
    n = lax.axis_size("gz")
    return lax.ppermute(x, "gz", [(i, i + 1) for i in range(n - 1)])


def down(x):
    n = lax.axis_size("gz")
    return lax.ppermute(x, "gz", [(i + 1, i) for i in range(n - 1)])


def reduce_chunk(other, own):
    total = own + to_core(other)
    from_prev = to_next(total[0:2])
    from_next = to_prev(total[2:4])
    from_prev, from_next = lax.optimization_barrier((from_prev, from_next))
    fwd_next = total[4:5] + from_prev[0:1]
    fwd_prev = total[5:6] + from_next[0:1]
    fwd_next, fwd_prev = lax.optimization_barrier((fwd_next, fwd_prev))
    last_a = to_next(fwd_next)
    last_b = to_prev(fwd_prev)
    last_a, last_b = lax.optimization_barrier((last_a, last_b))
    a = total[6:7] + from_next[1:2] + last_a
    b = total[7:8] + from_prev[1:2] + last_b
    return jnp.concatenate([a, b], 0)


def on_device(estimate, measured, lateral_x, lateral_y, depth_taps):
    view = lax.axis_index("view")
    core = lax.rem(view, 2)
    chip = lax.div(view, 2)
    recorded = measured[0]
    mx = lateral_x[0]
    my = lateral_y[0]

    nxt, prv, opp = (chip + 1) % 4, (chip + 3) % 4, (chip + 2) % 4
    order = jnp.stack([2 * opp, 2 * nxt + 1, 2 * opp + 1, 2 * prv, 2 * nxt, 2 * prv + 1, 2 * chip, 2 * chip + 1])
    starts = jnp.concatenate([core * 64 + 8 * order, (1 - core) * 64 + 8 * order, core[None]]).astype(jnp.int32)

    before = up(lax.dynamic_slice(estimate, (SLAB - FAR, core * 64, 0), (FAR, 64, N)))
    after = down(lax.dynamic_slice(estimate, (0, core * 64, 0), (FAR, 64, N)))
    tf, ta, x_all, x_halves, x_fwd, adj_x, fwd_y, adj_y, rec_own, rec_first, rec_last = prep(
        starts, depth_taps, mx, my, recorded
    )
    before, after, rec_first, rec_last = lax.optimization_barrier((before, after, rec_first, rec_last))
    rec_before = up(rec_last)
    rec_after = down(rec_first)
    before2, after2 = to_core(before), to_core(after)

    def log_sums(update, smooth):
        recs = (rec_before, rec_own, rec_after)
        owns, others = middle(LOTS[update], smooth, recs, tf, ta, adj_x, adj_y)
        return [reduce_chunk(other, own) for own, other in zip(owns, others)]

    mine = lax.dynamic_slice(estimate, (0, core * 64 + chip * 16, 0), (SLAB, 16, N))
    mine = jnp.stack([mine[:, :8], mine[:, 8:]], 0)

    (smooth_own,) = lateral([[estimate]], x_all, fwd_y)
    smooth_b, smooth_a = lateral([[before, before2], [after, after2]], x_halves, fwd_y)
    (log_sum,) = log_sums(0, (smooth_b, smooth_own, smooth_a))
    mine = mine * jnp.exp(log_sum / 8.0)

    prev_c, next_c = to_next(mine), to_prev(mine)
    b0, a0 = up(mine[:, SLAB - FAR :]), down(mine[:, :FAR])
    opp_a, opp_b = to_next(prev_c[0:1]), to_prev(next_c[1:2])
    sides = jnp.concatenate([prev_c, next_c], 0)
    b1, a1 = up(sides[:, SLAB - FAR :]), down(sides[:, :FAR])
    near = jnp.concatenate([mine, sides], 0)
    near2 = to_core(near)
    opp_c = jnp.concatenate([opp_a, opp_b], 0)
    b2, a2 = up(opp_c[:, SLAB - FAR :]), down(opp_c[:, :FAR])
    opp2 = to_core(opp_c)
    ends = jnp.concatenate([b0, b1, a0, a1], 0)
    ends2 = to_core(ends)
    tail = jnp.concatenate([b2, a2], 0)
    tail2 = to_core(tail)

    def in_order(near, opp_c):
        mine, prv, nxt = near[0:2], near[2:4], near[4:6]
        return [opp_c[0:1], nxt[1:2], opp_c[1:2], prv[0:1], nxt[0:1], prv[1:2], mine]

    (smooth_own,) = lateral([in_order(near, opp_c) + in_order(near2, opp2)], x_fwd, fwd_y)
    smooth_b, smooth_a = lateral(
        [
            in_order(ends[0:6], tail[0:2]) + in_order(ends2[0:6], tail2[0:2]),
            in_order(ends[6:12], tail[2:4]) + in_order(ends2[6:12], tail2[2:4]),
        ],
        x_fwd,
        fwd_y,
    )
    lots = []
    for k, log_sum in enumerate(log_sums(1, (smooth_b, smooth_own, smooth_a))):
        planes = log_sum.shape[1]
        chunk = mine[:, k * planes : (k + 1) * planes] * jnp.exp(log_sum / 8.0)
        prev_c, next_c = lax.optimization_barrier((to_next(chunk), to_prev(chunk)))
        opp_a, opp_b = to_next(prev_c[0:1]), to_prev(next_c[1:2])
        ours = jnp.concatenate([opp_a, next_c[1:2], opp_b, prev_c[0:1], next_c[0:1], prev_c[1:2], chunk], 0)
        lots.append([ours, to_core(ours)])
    return place(starts, lots)


def solution(mesh):
    return jax.shard_map(
        on_device,
        mesh=mesh,
        in_specs=(
            P("gz", None, None),
            P("view", "gz", None, None),
            P("view", None, None),
            P("view", None, None),
            P("view", None),
        ),
        out_specs=P("gz", None, None),
        check_vma=False,
    )
```

```python
import jax
import jax.numpy as jnp
from jax import lax
from jax.experimental import pallas as pl
from jax.experimental.pallas import tpu as pltpu
from jax.sharding import PartitionSpec as P

DEPTH = 33
HALF = 16
N = 128
SLAB = 48
FAR = 2 * HALF
F32 = jnp.float32
BF16 = jnp.bfloat16
MIB = 1024 * 1024
PITCH = 132
STEP = 16
LOTS = (1, 2)


def split(x):
    hi = x.astype(BF16)
    return hi, (x - hi.astype(F32)).astype(BF16)


def left_product(operand, x):
    hi, lo = split(x)
    out = jnp.dot(operand, jnp.concatenate([hi, lo], 0), preferred_element_type=F32)
    rows = operand.shape[0] // 2
    return out[:rows] + out[rows:]


def right_product(x, operand):
    hi, lo = split(x)
    out = jnp.dot(jnp.concatenate([hi, lo], 1), operand, preferred_element_type=F32)
    cols = operand.shape[1] // 2
    return out[:, :cols] + out[:, cols:]


def two_sided(planes, left, right):
    sides = [
        left_product(left, jnp.concatenate(planes[i : i + 2], 1)) for i in range(0, len(planes), 2)
    ]
    rows = jnp.concatenate([part for s in sides for part in (s[:, :N], s[:, N:])], 0)
    return right_product(rows, right)


def region_plane(refs, z):
    blocks = []
    for ref in refs:
        if len(ref.shape) == 3:
            blocks.append(ref[z])
        else:
            blocks.extend(ref[p, z] for p in range(ref.shape[0]))
    return jnp.concatenate(blocks, 0) if len(blocks) > 1 else blocks[0]


def lateral_kernel(counts, *refs):
    total = sum(c for c, _ in counts)
    ins, (left_ref, right_ref), outs = refs[:total], refs[total : total + 2], refs[total + 2 :]
    left = left_ref[...]
    right = right_ref[...]
    at = 0
    for (count, planes), out in zip(counts, outs):
        region = ins[at : at + count]
        at += count

        @pl.loop(0, planes // STEP)
        def _(i, region=region, out=out):
            zs = [STEP * i + j for j in range(STEP)]
            res = two_sided([region_plane(region, z) for z in zs], left, right)
            for j, z in enumerate(zs):
                out[pl.ds(z * PITCH, N), :] = res[j * N : j * N + N]


def lateral(regions, left, right):
    counts = []
    ins = []
    for region in regions:
        ref = region[0]
        counts.append((len(region), ref.shape[0] if ref.ndim == 3 else ref.shape[1]))
        ins.extend(region)
    planes = sum(p for _, p in counts)
    return pl.pallas_call(
        lambda *refs: lateral_kernel(counts, *refs),
        out_shape=[jax.ShapeDtypeStruct((p * PITCH, N), F32) for _, p in counts],
        in_specs=[pl.BlockSpec(memory_space=pltpu.VMEM)] * (len(ins) + 2),
        out_specs=[pl.BlockSpec(memory_space=pltpu.VMEM)] * len(counts),
        compiler_params=pltpu.CompilerParams(vmem_limit_bytes=24 * MIB),
        cost_estimate=pl.CostEstimate(flops=planes * 16 * N**3, bytes_accessed=planes * 8 * N * N, transcendentals=0),
        name="lateral",
    )(*ins, left, right)


def strided(refs, a):
    ends, own = refs
    parts = [(ends, 0, FAR), (own, 0, SLAB), (ends, FAR, FAR)]
    return jnp.concatenate([r[pl.ds(a + z * PITCH, n, stride=PITCH), :] for r, z, n in parts], 0)


def at_row(refs, a):
    return jnp.concatenate([r[a] for r in refs], 0)


def pair(pick, refs, a):
    return jnp.concatenate([pick(refs, a), pick(refs, a + 1)], 1)


def store_back(back, a, res):
    back[pl.ds(a, SLAB, stride=PITCH), :] = res[:, :N]
    back[pl.ds(a + 1, SLAB, stride=PITCH), :] = res[:, N:]


def logs_out(back, left_ref, right_ref, owns, others):
    left = left_ref[...]
    right = right_ref[...]
    begin = 0
    for own, other in zip(owns, others):
        planes = own.shape[1]
        step = 16 if planes % 16 == 0 else 8

        @pl.loop(0, planes // step)
        def _(i, own=own, other=other, begin=begin, step=step):
            zs = [step * i + j for j in range(step)]
            sides = [back[pl.ds((begin + z) * PITCH, N), :] for z in zs]
            logs = jnp.log(two_sided(sides, left, right))
            for j, z in enumerate(zs):
                for p in range(8):
                    own[p, z] = logs[j * N + 8 * p : j * N + 8 * p + 8]
                    other[p, z] = logs[j * N + 64 + 8 * p : j * N + 64 + 8 * p + 8]

        begin += planes


def middle_kernel(se, so, mb, mo, ma, tf_ref, ta_ref, left_ref, right_ref, *outs):
    outs, back = outs[:-1], outs[-1]
    lots = len(outs) // 2
    tf = tf_ref[...]
    ta = ta_ref[...]

    @pl.loop(0, N // STEP)
    def _(i):
        firsts = [STEP * i + j for j in range(0, STEP, 2)]
        blurred = [left_product(tf, pair(strided, (se, so), a)) for a in firsts]
        ratios = []
        for a, blur in zip(firsts, blurred):
            rec = pair(at_row, (mb, mo, ma), a)
            ratios.append(jnp.where(rec > 0, rec / blur, 0.0))
        for a, ratio in zip(firsts, ratios):
            store_back(back, a, left_product(ta, ratio))

    logs_out(back, left_ref, right_ref, outs[:lots], outs[lots:])


def middle(lots, smooth, recorded, tf, ta, left, right):
    ins = (*smooth, *recorded, tf, ta, left, right)
    half = jax.ShapeDtypeStruct((8, SLAB // lots, 8, N), F32)
    res = pl.pallas_call(
        middle_kernel,
        out_shape=[half] * (2 * lots),
        in_specs=[pl.BlockSpec(memory_space=pltpu.VMEM)] * len(ins),
        out_specs=[pl.BlockSpec(memory_space=pltpu.VMEM)] * (2 * lots),
        scratch_shapes=[pltpu.VMEM((SLAB * PITCH, N), F32)],
        compiler_params=pltpu.CompilerParams(vmem_limit_bytes=32 * MIB),
        cost_estimate=pl.CostEstimate(flops=8 * 10**9, bytes_accessed=15 * MIB, transcendentals=SLAB * N * N),
        name="middle",
    )(*ins)
    return res[:lots], res[lots:]


def operand_rows(m):
    hi, lo = split(m)
    return jnp.concatenate([hi, lo], 0)


def twice(m, axis):
    return jnp.concatenate([m, m], axis)


def operand_cols(m):
    hi, lo = split(twice(m, 0))
    return jnp.concatenate([hi, lo], 1)


def prep_kernel(
    starts, taps, mx_ref, my_ref, rec,
    tf, ta, x_all, x_halves, x_pieces, adj_x, fwd_y, adj_y, rec_t, rec_first, rec_last, xt_ref,
):
    def toeplitz(rows, cols, flip):
        i = lax.broadcasted_iota(jnp.int32, (rows, 2 * cols), 0)
        j = lax.broadcasted_iota(jnp.int32, (rows, 2 * cols), 1)
        diag = jnp.where(j >= cols, j - cols, j) - i
        out = jnp.zeros((rows, 2 * cols), F32)
        for k in range(DEPTH):
            out = jnp.where(diag == k, taps[0, DEPTH - 1 - k if flip else k], out)
        return out

    tf[...] = operand_rows(toeplitz(SLAB + 2 * HALF, SLAB + 2 * FAR, False))
    ta[...] = operand_rows(toeplitz(SLAB, SLAB + 2 * HALF, True))
    mx = mx_ref[...]
    my = my_ref[...]
    x_all[...] = operand_rows(twice(mx, 1))
    fwd_y[...] = operand_cols(my.T)
    adj_y[...] = operand_cols(my)
    xt_ref[...] = mx.T

    def row_blocks(rows):
        return jnp.concatenate([xt_ref[pl.ds(pl.multiple_of(r, 8), 8), :] for r in rows], 0)

    pieces = row_blocks([starts[p] for p in range(16)])
    adj_x[...] = operand_rows(twice(pieces, 1))
    x_pieces[...] = operand_rows(twice(pieces.T, 1))
    core = starts[16]
    halves = row_blocks([core * 64 + 8 * p for p in range(8)] + [64 - core * 64 + 8 * p for p in range(8)])
    x_halves[...] = operand_rows(twice(halves.T, 1))

    @pl.loop(0, N // 8)
    def _(i):
        at = pl.multiple_of(8 * i, 8)
        for zb in range(0, SLAB, 8):
            block = jnp.stack([rec[z, pl.ds(at, 8), :] for z in range(zb, zb + 8)], 0)
            block = jnp.swapaxes(block, 0, 1)
            for j in range(8):
                rec_t[at + j, zb : zb + 8, :] = block[j]
                if zb < HALF:
                    rec_first[at + j, zb : zb + 8, :] = block[j]
                if zb >= SLAB - HALF:
                    rec_last[at + j, zb - SLAB + HALF : zb - SLAB + HALF + 8, :] = block[j]


def prep(starts, taps, mx, my, rec):
    full = SLAB + 2 * HALF
    wide = SLAB + 2 * FAR
    square = jax.ShapeDtypeStruct((2 * N, 2 * N), BF16)
    edge = jax.ShapeDtypeStruct((N, HALF, N), F32)
    outs = [
        jax.ShapeDtypeStruct((2 * full, 2 * wide), BF16),
        jax.ShapeDtypeStruct((2 * SLAB, 2 * full), BF16),
        *[square] * 6,
        jax.ShapeDtypeStruct((N, SLAB, N), F32),
        edge,
        edge,
    ]
    vmem = pl.BlockSpec(memory_space=pltpu.VMEM)
    smem = pl.BlockSpec(memory_space=pltpu.SMEM)
    return pl.pallas_call(
        prep_kernel,
        out_shape=outs,
        in_specs=[smem, smem, vmem, vmem, vmem],
        out_specs=[vmem] * len(outs),
        scratch_shapes=[pltpu.VMEM((N, N), F32)],
        compiler_params=pltpu.CompilerParams(vmem_limit_bytes=20 * MIB),
        name="prep",
    )(starts, taps, mx, my, rec)


def place_kernel(lots, starts, *refs):
    out = refs[-1]
    per = (len(refs) - 1) // lots
    for k in range(lots):
        at = 0
        for ref in refs[k * per : k * per + per]:
            planes = ref.shape[1]
            for p in range(ref.shape[0]):
                begin = pl.multiple_of(starts[at], 8)
                out[k * planes : (k + 1) * planes, pl.ds(begin, 8), :] = ref[p]
                at += 1


def place(starts, lots):
    pieces = [p for lot in lots for p in lot]
    return pl.pallas_call(
        lambda *refs: place_kernel(len(lots), *refs),
        out_shape=jax.ShapeDtypeStruct((SLAB, N, N), F32),
        in_specs=[pl.BlockSpec(memory_space=pltpu.SMEM)] + [pl.BlockSpec(memory_space=pltpu.VMEM)] * len(pieces),
        out_specs=pl.BlockSpec(memory_space=pltpu.VMEM),
        compiler_params=pltpu.CompilerParams(vmem_limit_bytes=4 * MIB),
        name="place",
    )(starts, *pieces)


def to_core(x):
    return lax.ppermute(x, "view", [(i, i ^ 1) for i in range(8)])


def to_next(x):
    return lax.ppermute(x, "view", [(i, (i + 2) % 8) for i in range(8)])


def to_prev(x):
    return lax.ppermute(x, "view", [(i, (i - 2) % 8) for i in range(8)])


def up(x):
    n = lax.axis_size("gz")
    return lax.ppermute(x, "gz", [(i, i + 1) for i in range(n - 1)])


def down(x):
    n = lax.axis_size("gz")
    return lax.ppermute(x, "gz", [(i + 1, i) for i in range(n - 1)])


def cycle(x, step):
    n = lax.axis_size("gz")
    return lax.ppermute(x, "gz", [(i, (i + step) % n) for i in range(n)])


def reduce_chunk(other, own):
    total = own + to_core(other)
    from_prev = to_next(total[0:2])
    from_next = to_prev(total[2:4])
    from_prev, from_next = lax.optimization_barrier((from_prev, from_next))
    fwd_next = total[4:5] + from_prev[0:1]
    fwd_prev = total[5:6] + from_next[0:1]
    fwd_next, fwd_prev = lax.optimization_barrier((fwd_next, fwd_prev))
    last_a = to_next(fwd_next)
    last_b = to_prev(fwd_prev)
    last_a, last_b = lax.optimization_barrier((last_a, last_b))
    a = total[6:7] + from_next[1:2] + last_a
    b = total[7:8] + from_prev[1:2] + last_b
    return jnp.concatenate([a, b], 0)


def on_device(estimate, measured, lateral_x, lateral_y, depth_taps):
    view = lax.axis_index("view")
    core = lax.rem(view, 2)
    chip = lax.div(view, 2)
    recorded = measured[0]
    mx = lateral_x[0]
    my = lateral_y[0]

    nxt, prv, opp = (chip + 1) % 4, (chip + 3) % 4, (chip + 2) % 4
    order = jnp.stack([2 * opp, 2 * nxt + 1, 2 * opp + 1, 2 * prv, 2 * nxt, 2 * prv + 1, 2 * chip, 2 * chip + 1])
    starts = jnp.concatenate([core * 64 + 8 * order, (1 - core) * 64 + 8 * order, core[None]]).astype(jnp.int32)

    before = cycle(lax.dynamic_slice(estimate, (SLAB - FAR, core * 64, 0), (FAR, 64, N)), 1)
    after = cycle(lax.dynamic_slice(estimate, (0, core * 64, 0), (FAR, 64, N)), -1)
    tf, ta, x_all, x_halves, x_fwd, adj_x, fwd_y, adj_y, rec_own, rec_first, rec_last = prep(
        starts, depth_taps, mx, my, recorded
    )
    before, after, rec_first, rec_last = lax.optimization_barrier((before, after, rec_first, rec_last))
    slab = lax.axis_index("gz")
    inside = slab > 0, slab < lax.axis_size("gz") - 1

    def clip(before, after):
        return jnp.where(inside[0], before, 0.0), jnp.where(inside[1], after, 0.0)

    rec_before, rec_after = clip(cycle(rec_last, 1), cycle(rec_first, -1))
    ends = jnp.concatenate(clip(before, after), 0)
    ends2 = to_core(ends)

    def log_sums(update, smooth):
        recs = (rec_before, rec_own, rec_after)
        owns, others = middle(LOTS[update], smooth, recs, tf, ta, adj_x, adj_y)
        return [reduce_chunk(other, own) for own, other in zip(owns, others)]

    mine = lax.dynamic_slice(estimate, (0, core * 64 + chip * 16, 0), (SLAB, 16, N))
    mine = jnp.stack([mine[:, :8], mine[:, 8:]], 0)

    (smooth_own,) = lateral([[estimate]], x_all, fwd_y)
    (smooth_ends,) = lateral([[ends, ends2]], x_halves, fwd_y)
    (log_sum,) = log_sums(0, (smooth_ends, smooth_own))
    mine = mine * jnp.exp(log_sum / 8.0)

    prev_c, next_c = to_next(mine), to_prev(mine)
    b0, a0 = up(mine[:, SLAB - FAR :]), down(mine[:, :FAR])
    opp_a, opp_b = to_next(prev_c[0:1]), to_prev(next_c[1:2])
    sides = jnp.concatenate([prev_c, next_c], 0)
    b1, a1 = up(sides[:, SLAB - FAR :]), down(sides[:, :FAR])
    near = jnp.concatenate([mine, sides], 0)
    near2 = to_core(near)
    opp_c = jnp.concatenate([opp_a, opp_b], 0)
    b2, a2 = up(opp_c[:, SLAB - FAR :]), down(opp_c[:, :FAR])
    opp2 = to_core(opp_c)
    ends = jnp.concatenate([jnp.concatenate([b0, a0], 1), jnp.concatenate([b1, a1], 1)], 0)
    ends2 = to_core(ends)
    tail = jnp.concatenate([b2, a2], 1)
    tail2 = to_core(tail)

    def in_order(near, opp_c):
        mine, prv, nxt = near[0:2], near[2:4], near[4:6]
        return [opp_c[0:1], nxt[1:2], opp_c[1:2], prv[0:1], nxt[0:1], prv[1:2], mine]

    (smooth_own,) = lateral([in_order(near, opp_c) + in_order(near2, opp2)], x_fwd, fwd_y)
    (smooth_ends,) = lateral([in_order(ends, tail) + in_order(ends2, tail2)], x_fwd, fwd_y)
    lots = []
    for k, log_sum in enumerate(log_sums(1, (smooth_ends, smooth_own))):
        planes = log_sum.shape[1]
        chunk = mine[:, k * planes : (k + 1) * planes] * jnp.exp(log_sum / 8.0)
        prev_c, next_c = lax.optimization_barrier((to_next(chunk), to_prev(chunk)))
        opp_a, opp_b = to_next(prev_c[0:1]), to_prev(next_c[1:2])
        ours = jnp.concatenate([opp_a, next_c[1:2], opp_b, prev_c[0:1], next_c[0:1], prev_c[1:2], chunk], 0)
        lots.append([ours, to_core(ours)])
    return place(starts, lots)


def solution(mesh):
    return jax.shard_map(
        on_device,
        mesh=mesh,
        in_specs=(
            P("gz", None, None),
            P("view", "gz", None, None),
            P("view", None, None),
            P("view", None, None),
            P("view", None),
        ),
        out_specs=P("gz", None, None),
        check_vma=False,
    )
```

```python
import jax
import jax.numpy as jnp
from jax import lax
from jax.experimental import pallas as pl
from jax.experimental.pallas import tpu as pltpu
from jax.sharding import PartitionSpec as P

DEPTH = 33
HALF = 16
N = 128
SLAB = 48
FAR = 2 * HALF
F32 = jnp.float32
BF16 = jnp.bfloat16
MIB = 1024 * 1024
PITCH = 132
STEP = 16
LOTS = (1, 2)


def split(x):
    hi = x.astype(BF16)
    return hi, (x - hi.astype(F32)).astype(BF16)


def left_product(operand, x):
    hi, lo = split(x)
    out = jnp.dot(operand, jnp.concatenate([hi, lo], 0), preferred_element_type=F32)
    rows = operand.shape[0] // 2
    return out[:rows] + out[rows:]


def right_product(x, operand):
    hi, lo = split(x)
    out = jnp.dot(jnp.concatenate([hi, lo], 1), operand, preferred_element_type=F32)
    cols = operand.shape[1] // 2
    return out[:, :cols] + out[:, cols:]


def two_sided(planes, left, right):
    sides = [
        left_product(left, jnp.concatenate(planes[i : i + 2], 1)) for i in range(0, len(planes), 2)
    ]
    rows = jnp.concatenate([part for s in sides for part in (s[:, :N], s[:, N:])], 0)
    return right_product(rows, right)


def region_plane(refs, z):
    blocks = []
    for ref in refs:
        if len(ref.shape) == 3:
            blocks.append(ref[z])
        else:
            blocks.extend(ref[p, z] for p in range(ref.shape[0]))
    return jnp.concatenate(blocks, 0) if len(blocks) > 1 else blocks[0]


def lateral_kernel(counts, step, *refs):
    total = sum(c for c, _ in counts)
    ins, (left_ref, right_ref), outs = refs[:total], refs[total : total + 2], refs[total + 2 :]
    left = left_ref[...]
    right = right_ref[...]
    at = 0
    for (count, planes), out in zip(counts, outs):
        region = ins[at : at + count]
        at += count

        @pl.loop(0, planes // step)
        def _(i, region=region, out=out):
            zs = [step * i + j for j in range(step)]
            res = two_sided([region_plane(region, z) for z in zs], left, right)
            for j, z in enumerate(zs):
                out[pl.ds(z * PITCH, N), :] = res[j * N : j * N + N]


def lateral(regions, left, right, step=STEP):
    counts = []
    ins = []
    for region in regions:
        ref = region[0]
        counts.append((len(region), ref.shape[0] if ref.ndim == 3 else ref.shape[1]))
        ins.extend(region)
    planes = sum(p for _, p in counts)
    return pl.pallas_call(
        lambda *refs: lateral_kernel(counts, step, *refs),
        out_shape=[jax.ShapeDtypeStruct((p * PITCH, N), F32) for _, p in counts],
        in_specs=[pl.BlockSpec(memory_space=pltpu.VMEM)] * (len(ins) + 2),
        out_specs=[pl.BlockSpec(memory_space=pltpu.VMEM)] * len(counts),
        compiler_params=pltpu.CompilerParams(vmem_limit_bytes=24 * MIB),
        cost_estimate=pl.CostEstimate(flops=planes * 16 * N**3, bytes_accessed=planes * 8 * N * N, transcendentals=0),
        name="lateral",
    )(*ins, left, right)


def strided(refs, a):
    return jnp.concatenate([r[pl.ds(a, r.shape[0] // PITCH, stride=PITCH), :] for r in refs], 0)


def at_row(refs, a):
    return jnp.concatenate([r[a] for r in refs], 0)


def pair(pick, refs, a):
    return jnp.concatenate([pick(refs, a), pick(refs, a + 1)], 1)


def store_back(back, a, res):
    back[pl.ds(a, SLAB, stride=PITCH), :] = res[:, :N]
    back[pl.ds(a + 1, SLAB, stride=PITCH), :] = res[:, N:]


def logs_out(back, left_ref, right_ref, owns, others):
    left = left_ref[...]
    right = right_ref[...]
    begin = 0
    for own, other in zip(owns, others):
        planes = own.shape[1]
        step = 16 if planes % 16 == 0 else 8

        @pl.loop(0, planes // step)
        def _(i, own=own, other=other, begin=begin, step=step):
            zs = [step * i + j for j in range(step)]
            sides = [back[pl.ds((begin + z) * PITCH, N), :] for z in zs]
            logs = jnp.log(two_sided(sides, left, right))
            for j, z in enumerate(zs):
                for p in range(8):
                    own[p, z] = logs[j * N + 8 * p : j * N + 8 * p + 8]
                    other[p, z] = logs[j * N + 64 + 8 * p : j * N + 64 + 8 * p + 8]

        begin += planes


def middle_kernel(sb, so, sa, mb, mo, ma, tf_ref, ta_ref, left_ref, right_ref, *outs):
    outs, back = outs[:-1], outs[-1]
    lots = len(outs) // 2
    tf = tf_ref[...]
    ta = ta_ref[...]

    @pl.loop(0, N // STEP)
    def _(i):
        firsts = [STEP * i + j for j in range(0, STEP, 2)]
        blurred = [left_product(tf, pair(strided, (sb, so, sa), a)) for a in firsts]
        ratios = []
        for a, blur in zip(firsts, blurred):
            rec = pair(at_row, (mb, mo, ma), a)
            ratios.append(jnp.where(rec > 0, rec / blur, 0.0))
        for a, ratio in zip(firsts, ratios):
            store_back(back, a, left_product(ta, ratio))

    logs_out(back, left_ref, right_ref, outs[:lots], outs[lots:])


def middle(lots, smooth, recorded, tf, ta, left, right):
    ins = (*smooth, *recorded, tf, ta, left, right)
    half = jax.ShapeDtypeStruct((8, SLAB // lots, 8, N), F32)
    res = pl.pallas_call(
        middle_kernel,
        out_shape=[half] * (2 * lots),
        in_specs=[pl.BlockSpec(memory_space=pltpu.VMEM)] * len(ins),
        out_specs=[pl.BlockSpec(memory_space=pltpu.VMEM)] * (2 * lots),
        scratch_shapes=[pltpu.VMEM((SLAB * PITCH, N), F32)],
        compiler_params=pltpu.CompilerParams(vmem_limit_bytes=32 * MIB),
        cost_estimate=pl.CostEstimate(flops=8 * 10**9, bytes_accessed=15 * MIB, transcendentals=SLAB * N * N),
        name="middle",
    )(*ins)
    return res[:lots], res[lots:]


def operand_rows(m):
    hi, lo = split(m)
    return jnp.concatenate([hi, lo], 0)


def twice(m, axis):
    return jnp.concatenate([m, m], axis)


def operand_cols(m):
    hi, lo = split(twice(m, 0))
    return jnp.concatenate([hi, lo], 1)


def prep_kernel(
    starts, taps, mx_ref, my_ref, rec,
    tf, ta, x_all, x_halves, x_pieces, adj_x, fwd_y, adj_y, rec_t, rec_first, rec_last, xt_ref,
):
    def toeplitz(rows, cols, flip):
        i = lax.broadcasted_iota(jnp.int32, (rows, 2 * cols), 0)
        j = lax.broadcasted_iota(jnp.int32, (rows, 2 * cols), 1)
        diag = jnp.where(j >= cols, j - cols, j) - i
        out = jnp.zeros((rows, 2 * cols), F32)
        for k in range(DEPTH):
            out = jnp.where(diag == k, taps[0, DEPTH - 1 - k if flip else k], out)
        return out

    tf[...] = operand_rows(toeplitz(SLAB + 2 * HALF, SLAB + 2 * FAR, False))
    ta[...] = operand_rows(toeplitz(SLAB, SLAB + 2 * HALF, True))
    mx = mx_ref[...]
    my = my_ref[...]
    x_all[...] = operand_rows(twice(mx, 1))
    fwd_y[...] = operand_cols(my.T)
    adj_y[...] = operand_cols(my)
    xt_ref[...] = mx.T

    def row_blocks(rows):
        return jnp.concatenate([xt_ref[pl.ds(pl.multiple_of(r, 8), 8), :] for r in rows], 0)

    pieces = row_blocks([starts[p] for p in range(16)])
    adj_x[...] = operand_rows(twice(pieces, 1))
    x_pieces[...] = operand_rows(twice(pieces.T, 1))
    core = starts[16]
    halves = row_blocks([core * 64 + 8 * p for p in range(8)] + [64 - core * 64 + 8 * p for p in range(8)])
    x_halves[...] = operand_rows(twice(halves.T, 1))

    @pl.loop(0, N // 8)
    def _(i):
        at = pl.multiple_of(8 * i, 8)
        for zb in range(0, SLAB, 8):
            block = jnp.stack([rec[z, pl.ds(at, 8), :] for z in range(zb, zb + 8)], 0)
            block = jnp.swapaxes(block, 0, 1)
            for j in range(8):
                rec_t[at + j, zb : zb + 8, :] = block[j]
                if zb < HALF:
                    rec_first[at + j, zb : zb + 8, :] = block[j]
                if zb >= SLAB - HALF:
                    rec_last[at + j, zb - SLAB + HALF : zb - SLAB + HALF + 8, :] = block[j]


def prep(starts, taps, mx, my, rec):
    full = SLAB + 2 * HALF
    wide = SLAB + 2 * FAR
    square = jax.ShapeDtypeStruct((2 * N, 2 * N), BF16)
    edge = jax.ShapeDtypeStruct((N, HALF, N), F32)
    outs = [
        jax.ShapeDtypeStruct((2 * full, 2 * wide), BF16),
        jax.ShapeDtypeStruct((2 * SLAB, 2 * full), BF16),
        *[square] * 6,
        jax.ShapeDtypeStruct((N, SLAB, N), F32),
        edge,
        edge,
    ]
    vmem = pl.BlockSpec(memory_space=pltpu.VMEM)
    smem = pl.BlockSpec(memory_space=pltpu.SMEM)
    return pl.pallas_call(
        prep_kernel,
        out_shape=outs,
        in_specs=[smem, smem, vmem, vmem, vmem],
        out_specs=[vmem] * len(outs),
        scratch_shapes=[pltpu.VMEM((N, N), F32)],
        compiler_params=pltpu.CompilerParams(vmem_limit_bytes=20 * MIB),
        name="prep",
    )(starts, taps, mx, my, rec)


def place_kernel(lots, starts, *refs):
    out = refs[-1]
    per = (len(refs) - 1) // lots
    for k in range(lots):
        at = 0
        for ref in refs[k * per : k * per + per]:
            planes = ref.shape[1]
            for p in range(ref.shape[0]):
                begin = pl.multiple_of(starts[at], 8)
                out[k * planes : (k + 1) * planes, pl.ds(begin, 8), :] = ref[p]
                at += 1


def place(starts, lots):
    pieces = [p for lot in lots for p in lot]
    return pl.pallas_call(
        lambda *refs: place_kernel(len(lots), *refs),
        out_shape=jax.ShapeDtypeStruct((SLAB, N, N), F32),
        in_specs=[pl.BlockSpec(memory_space=pltpu.SMEM)] + [pl.BlockSpec(memory_space=pltpu.VMEM)] * len(pieces),
        out_specs=pl.BlockSpec(memory_space=pltpu.VMEM),
        compiler_params=pltpu.CompilerParams(vmem_limit_bytes=4 * MIB),
        name="place",
    )(starts, *pieces)


def to_core(x):
    return lax.ppermute(x, "view", [(i, i ^ 1) for i in range(8)])


def to_next(x):
    return lax.ppermute(x, "view", [(i, (i + 2) % 8) for i in range(8)])


def to_prev(x):
    return lax.ppermute(x, "view", [(i, (i - 2) % 8) for i in range(8)])


def up(x):
    n = lax.axis_size("gz")
    return lax.ppermute(x, "gz", [(i, i + 1) for i in range(n - 1)])


def down(x):
    n = lax.axis_size("gz")
    return lax.ppermute(x, "gz", [(i + 1, i) for i in range(n - 1)])


def cycle(x, step):
    n = lax.axis_size("gz")
    return lax.ppermute(x, "gz", [(i, (i + step) % n) for i in range(n)])


def reduce_chunk(other, own):
    total = own + to_core(other)
    from_prev = to_next(total[0:2])
    from_next = to_prev(total[2:4])
    from_prev, from_next = lax.optimization_barrier((from_prev, from_next))
    fwd_next = total[4:5] + from_prev[0:1]
    fwd_prev = total[5:6] + from_next[0:1]
    fwd_next, fwd_prev = lax.optimization_barrier((fwd_next, fwd_prev))
    last_a = to_next(fwd_next)
    last_b = to_prev(fwd_prev)
    last_a, last_b = lax.optimization_barrier((last_a, last_b))
    a = total[6:7] + from_next[1:2] + last_a
    b = total[7:8] + from_prev[1:2] + last_b
    return jnp.concatenate([a, b], 0)


def on_device(estimate, measured, lateral_x, lateral_y, depth_taps):
    view = lax.axis_index("view")
    core = lax.rem(view, 2)
    chip = lax.div(view, 2)
    recorded = measured[0]
    mx = lateral_x[0]
    my = lateral_y[0]

    nxt, prv, opp = (chip + 1) % 4, (chip + 3) % 4, (chip + 2) % 4
    order = jnp.stack([2 * opp, 2 * nxt + 1, 2 * opp + 1, 2 * prv, 2 * nxt, 2 * prv + 1, 2 * chip, 2 * chip + 1])
    starts = jnp.concatenate([core * 64 + 8 * order, (1 - core) * 64 + 8 * order, core[None]]).astype(jnp.int32)

    before = cycle(lax.dynamic_slice(estimate, (SLAB - FAR, core * 64, 0), (FAR, 64, N)), 1)
    after = cycle(lax.dynamic_slice(estimate, (0, core * 64, 0), (FAR, 64, N)), -1)
    tf, ta, x_all, x_halves, x_fwd, adj_x, fwd_y, adj_y, rec_own, rec_first, rec_last = prep(
        starts, depth_taps, mx, my, recorded
    )
    before, after, rec_first, rec_last = lax.optimization_barrier((before, after, rec_first, rec_last))
    slab = lax.axis_index("gz")

    def clip(before, after):
        there = slab > 0, slab < lax.axis_size("gz") - 1
        return jnp.where(there[0], before, 0.0), jnp.where(there[1], after, 0.0)

    rec_before, rec_after = cycle(rec_last, 1), cycle(rec_first, -1)
    before, after = clip(before, after)
    before2, after2 = to_core(before), to_core(after)

    def log_sums(update, smooth):
        recs = (rec_before, rec_own, rec_after)
        owns, others = middle(LOTS[update], smooth, recs, tf, ta, adj_x, adj_y)
        return [reduce_chunk(other, own) for own, other in zip(owns, others)]

    mine = lax.dynamic_slice(estimate, (0, core * 64 + chip * 16, 0), (SLAB, 16, N))
    mine = jnp.stack([mine[:, :8], mine[:, 8:]], 0)

    (smooth_own,) = lateral([[estimate]], x_all, fwd_y, 8)
    smooth_b, smooth_a = lateral([[before, before2], [after, after2]], x_halves, fwd_y, 8)
    rec_before, rec_after, smooth_b, smooth_a = lax.optimization_barrier((rec_before, rec_after, smooth_b, smooth_a))
    rec_before, rec_after = clip(rec_before, rec_after)
    (log_sum,) = log_sums(0, (smooth_b, smooth_own, smooth_a))
    mine = mine * jnp.exp(log_sum / 8.0)

    prev_c, next_c = to_next(mine), to_prev(mine)
    b0, a0 = up(mine[:, SLAB - FAR :]), down(mine[:, :FAR])
    opp_a, opp_b = to_next(prev_c[0:1]), to_prev(next_c[1:2])
    sides = jnp.concatenate([prev_c, next_c], 0)
    b1, a1 = up(sides[:, SLAB - FAR :]), down(sides[:, :FAR])
    near = jnp.concatenate([mine, sides], 0)
    near2 = to_core(near)
    opp_c = jnp.concatenate([opp_a, opp_b], 0)
    b2, a2 = up(opp_c[:, SLAB - FAR :]), down(opp_c[:, :FAR])
    opp2 = to_core(opp_c)
    ends = jnp.concatenate([b0, b1, a0, a1], 0)
    ends2 = to_core(ends)
    tail = jnp.concatenate([b2, a2], 0)
    tail2 = to_core(tail)

    def in_order(near, opp_c):
        mine, prv, nxt = near[0:2], near[2:4], near[4:6]
        return [opp_c[0:1], nxt[1:2], opp_c[1:2], prv[0:1], nxt[0:1], prv[1:2], mine]

    (smooth_own,) = lateral([in_order(near, opp_c) + in_order(near2, opp2)], x_fwd, fwd_y)
    smooth_b, smooth_a = lateral(
        [
            in_order(ends[0:6], tail[0:2]) + in_order(ends2[0:6], tail2[0:2]),
            in_order(ends[6:12], tail[2:4]) + in_order(ends2[6:12], tail2[2:4]),
        ],
        x_fwd,
        fwd_y,
    )
    log_sum = jnp.concatenate(log_sums(1, (smooth_b, smooth_own, smooth_a)), 1)
    mine = mine * jnp.exp(log_sum / 8.0)
    prev_c, next_c = lax.optimization_barrier((to_next(mine), to_prev(mine)))
    near = jnp.concatenate([mine, prev_c, next_c], 0)
    near2 = to_core(near)
    opp_c = jnp.concatenate([to_next(prev_c[0:1]), to_prev(next_c[1:2])], 0)
    opp2 = to_core(opp_c)
    return place(starts, [in_order(near, opp_c) + in_order(near2, opp2)])


def solution(mesh):
    return jax.shard_map(
        on_device,
        mesh=mesh,
        in_specs=(
            P("gz", None, None),
            P("view", "gz", None, None),
            P("view", None, None),
            P("view", None, None),
            P("view", None),
        ),
        out_specs=P("gz", None, None),
        check_vma=False,
    )
```
